512 devices in a mesh: lead: 16 (over z, core), lat: 32 (over x, y).
Axes of the slice: x: 4, y: 8, z: 8, core: 2. Of those that a mesh axis runs over, the one named last changes fastest.
Arguments:
- window: bfloat16 [16, 96, 192, 768], P('lead', 'lat'), may hold values from -10 to 10
- noise_level: float32 [16], replicated, may hold values from 0.1 to 10
- keep_ratio: float32 [16], replicated, may hold values from 0.3 to 0.95
- norm_gains: float32 [3, 768], replicated, may hold values from 0.5 to 1.5
- w_qkv: bfloat16 [768, 1152], replicated, may hold values from -0.19921875 to 0.19921875
- w_out: bfloat16 [384, 768], replicated, may hold values from -0.3125 to 0.3125
- spectral_filter: bfloat16 [96, 768], replicated, may hold values from -2.5 to 2.5
- w_in: bfloat16 [1536, 768], P('lead'), may hold values from -0.21875 to 0.21875
- w_down: bfloat16 [1536, 768], P('lead'), may hold values from -0.15625 to 0.15625
Outputs:
- next_window: bfloat16 [16, 96, 192, 768], P('lead', 'lat')
The draws below stay inside these ranges and needn't reach their ends.
All inputs are finite; a program needn't handle non-finite values.
Results may differ from the reference program's by a relative error of at most 0.011.
Values may be sent and summed in bfloat16 or wider, within the bound.
No kernel may reach another device: no remote copies, remote signals or barrier semaphores. Data moves between devices by JAX's collectives and lax.ppermute only.
A program may use at most 64 MiB of HBM per device.

```python
import math
import jax
import jax.numpy as jnp
import numpy as np
from jax import lax

WIDTH = 768
HEADS = 6
HEAD_DIM = 64
FF_UNITS = 1536
NLON = 192
FRAMES = 16
NLAT = 96
LMAX = 96


def longitude_wave(key, amp_low, amp_high, scale_factor):
    subkeys = jax.random.split(key, 3)
    lowest = max(1, LMAX // 16)
    highest = max(lowest + 1, LMAX // 5)
    order_list = jax.random.randint(subkeys[0], (WIDTH,), lowest, highest + 1)
    products = jnp.mod(jnp.arange(NLON, dtype=jnp.int32)[:, None] * order_list[None, :], NLON)
    angles = 2.0 * math.pi / NLON * products.astype(jnp.float32)
    phases = jax.random.uniform(subkeys[1], (FRAMES, NLAT, 1, WIDTH), jnp.float32, -math.pi, math.pi)
    amplitudes = jax.random.uniform(subkeys[2], (FRAMES, NLAT, 1, WIDTH), jnp.float32, amp_low, amp_high)
    return scale_factor * amplitudes * jnp.cos(angles[None, None] + phases)


def draw_window(key, part):
    key = jax.random.fold_in(key, 11)
    subkeys = jax.random.split(key, 5)
    full_shape = (FRAMES, NLAT, NLON, WIDTH)
    noise_part = jnp.clip(jax.random.normal(subkeys[0], full_shape, jnp.float32), -5.0, 5.0)
    values = noise_part + longitude_wave(subkeys[4], 0.3, 1.7, 2.5)
    return values.astype(jnp.bfloat16)


def draw_w_qkv(key, part):
    key = jax.random.fold_in(key, 12)
    subkeys = jax.random.split(key, 1)
    columns = 3 * HEADS * HEAD_DIM
    matrix = jnp.clip(jax.random.normal(subkeys[0], (WIDTH, columns), jnp.float32), -5.0, 5.0) * WIDTH ** (-0.5)
    matrix = jnp.clip(matrix, -0.19921875, 0.19921875)
    return matrix.astype(jnp.bfloat16)


def draw_spectral_filter(key, part):
    key = jax.random.fold_in(key, 13)
    subkeys = jax.random.split(key, 2)
    degrees = jnp.arange(LMAX, dtype=jnp.float32)[:, None]
    magnitude = jax.random.uniform(subkeys[0], (LMAX, WIDTH), jnp.float32, 0.5, 1.0) * (1.0 + 1.5 * degrees / LMAX)
    signs = jnp.where(jax.random.bernoulli(subkeys[1], 0.5, (LMAX, WIDTH)), 1.0, -1.0)
    return (signs * magnitude).astype(jnp.bfloat16)


def levels(stream_key, dims, shards, least, largest):
    loudness, own = 1.0, jax.random.fold_in(stream_key, 6)
    for axis_at, blocks in shards:
        heights = jnp.exp(jax.random.uniform(jax.random.fold_in(own, axis_at), (blocks,), jnp.float32, least / len(shards), largest / len(shards)))
        loudness = loudness * jnp.repeat(heights, dims[axis_at] // blocks).reshape([-1 if axis == axis_at else 1 for axis in range(len(dims))])
    return loudness


def noise(rng, shape, scale, reach, shards=(), kind=jnp.bfloat16):
    result = jax.random.normal(rng, shape, jnp.float32) * scale
    if len(shards) > 0:
        result = levels(rng, shape, shards, -0.22, 0.18) * result
    return jnp.clip(result, min=-reach, max=reach).astype(kind)


def setup_inputs(seed: int = 0) -> dict:
    key_list = jax.random.split(jax.random.key(seed), 10)
    window = draw_window(jax.random.fold_in(key_list[9], 71), 0)
    noise_level = jnp.clip(jnp.exp(jax.random.uniform(key_list[1], (FRAMES,), jnp.float32, math.log(0.1), math.log(10.0))), 0.1, 10.0)
    keep_ratio = jnp.clip(jax.random.uniform(key_list[2], (FRAMES,), jnp.float32, 0.3, 0.95), 0.3, 0.95)
    norm_gains = jnp.clip(1.0 + 0.1 * jax.random.normal(key_list[3], (3, WIDTH), jnp.float32), 0.5, 1.5)
    w_qkv = draw_w_qkv(jax.random.fold_in(key_list[9], 71), 0)
    w_out = noise(key_list[5], (HEADS * HEAD_DIM, WIDTH), (HEADS * HEAD_DIM) ** -0.5, 0.3125)
    spectral_filter = draw_spectral_filter(jax.random.fold_in(key_list[9], 71), 0)
    w_in = noise(key_list[7], (FF_UNITS, WIDTH), WIDTH ** -0.5, 0.21875, ((0, 16),))
    w_down = noise(key_list[8], (FF_UNITS, WIDTH), FF_UNITS ** -0.5, 0.15625, ((0, 16),))
    return dict(window=window, noise_level=noise_level, keep_ratio=keep_ratio, norm_gains=norm_gains, w_qkv=w_qkv, w_out=w_out, spectral_filter=spectral_filter, w_in=w_in, w_down=w_down)


def spectral_tables(nlat, nlon, lmax):
    colatitude = np.pi * (np.arange(nlat) + 0.5) / nlat
    cosines = np.cos(colatitude)
    sine_rows = np.sin(colatitude)
    legendre = np.zeros((lmax, lmax, nlat))
    for order_m in range(lmax):
        counter = np.arange(1, order_m + 1)
        log_part = 0.5 * np.log((2 * order_m + 1) / (4 * np.pi)) + 0.5 * np.sum(np.log((2 * counter - 1) / (2 * counter))) + order_m * np.log(sine_rows)
        diagonal_value = (-1.0) ** order_m * np.exp(log_part)
        legendre[order_m, order_m] = diagonal_value
        if order_m + 1 < lmax:
            legendre[order_m, order_m + 1] = cosines * np.sqrt(2 * order_m + 3) * diagonal_value
        for degree_l in range(order_m + 2, lmax):
            factor_a = np.sqrt((4.0 * degree_l * degree_l - 1) / (degree_l * degree_l - order_m * order_m))
            factor_b = np.sqrt(((degree_l - 1.0) ** 2 - order_m * order_m) / (4.0 * (degree_l - 1) ** 2 - 1))
            legendre[order_m, degree_l] = factor_a * (cosines * legendre[order_m, degree_l - 1] - factor_b * legendre[order_m, degree_l - 2])
    quadrature = sine_rows * (np.pi / nlat) * (2 * np.pi / nlon)
    doubling = np.where(np.arange(lmax) == 0, 1.0, 2.0)
    angles = 2 * np.pi * np.outer(np.arange(nlon), np.arange(lmax)) / nlon
    return (jnp.asarray(legendre, jnp.float32), jnp.asarray(quadrature, jnp.float32), jnp.asarray(doubling, jnp.float32), jnp.asarray(np.cos(angles), jnp.float32), jnp.asarray(np.sin(angles), jnp.float32))

def rms_scale(values, gain):
    return values * lax.rsqrt(lax.optimization_barrier(jnp.mean(values * values, axis=-1, keepdims=True)) + 1e-05) * gain

def causal_mix(queries, keys, values_in):
    frames = queries.shape[0]
    head_dim = queries.shape[-1]
    scores = jnp.einsum('fphd,gphd->fgph', queries.astype(jnp.float32), keys.astype(jnp.float32)) / np.sqrt(head_dim)
    allowed = (jnp.arange(frames)[None, :] <= jnp.arange(frames)[:, None])[:, :, None, None]
    highest = lax.optimization_barrier(jnp.max(jnp.where(allowed, scores, -1e+30), axis=1, keepdims=True))
    expo = jnp.where(allowed, jnp.exp(jnp.minimum(scores - highest, 0.0)), 0.0)
    total = lax.optimization_barrier(jnp.sum(expo, axis=1))
    weights = expo.astype(jnp.bfloat16)
    mixed = jnp.einsum('fgph,gphd->fphd', weights.astype(jnp.float32), values_in.astype(jnp.float32))
    mixed = mixed / total[:, :, :, None]
    return mixed.astype(jnp.bfloat16).reshape(frames, queries.shape[1], -1)

def spectral_filter_grid(base, legendre, quadrature, doubling, cos_table, sin_table, filter_both):
    width = base.shape[-1]
    precise = lax.Precision.HIGHEST
    real_part = jnp.einsum('jkc,km->jmc', base, cos_table, precision=precise)
    imag_part = -jnp.einsum('jkc,km->jmc', base, sin_table, precision=precise)
    spectra = jnp.concatenate([real_part, imag_part], axis=-1)
    weighted = spectra * quadrature[:, None, None]
    coeffs = jnp.einsum('mlj,jmc->mlc', legendre, weighted, precision=precise) * filter_both[None]
    back = jnp.einsum('mlj,mlc->jmc', legendre, coeffs, precision=precise) * doubling[None, :, None]
    grid = jnp.einsum('jmc,km->jkc', back[..., :width], cos_table, precision=precise)
    return grid - jnp.einsum('jmc,km->jkc', back[..., width:], sin_table, precision=precise)

def reference(window, noise_level, keep_ratio, norm_gains, w_qkv, w_out, spectral_filter, w_in, w_down):
    frames, nlat, nlon, width = window.shape
    lmax = spectral_filter.shape[0]
    points = nlat * nlon
    legendre, quadrature, doubling, cos_table, sin_table = spectral_tables(nlat, nlon, lmax)
    filter_both = jnp.concatenate([spectral_filter, spectral_filter], axis=1).astype(jnp.float32)
    state = window.astype(jnp.float32).reshape(frames, points, width)
    scaled = state * lax.rsqrt(1.0 + noise_level * noise_level)[:, None, None]
    normed = rms_scale(scaled, norm_gains[0]).astype(jnp.bfloat16)
    projected = jnp.dot(normed.reshape(frames * points, width), w_qkv, preferred_element_type=jnp.float32)
    projected = projected.astype(jnp.bfloat16).reshape(frames, points, 3, HEADS, HEAD_DIM)
    mixed = causal_mix(projected[:, :, 0], projected[:, :, 1], projected[:, :, 2])
    ratios = jnp.where(jnp.arange(frames) == 0, 0.0, keep_ratio).astype(jnp.float32)

    def one_frame(items):
        scaled_frame, mixed_frame, state_frame, ratio = items
        first = scaled_frame + jnp.dot(mixed_frame, w_out, preferred_element_type=jnp.float32)
        base = rms_scale(first, norm_gains[1]).reshape(nlat, nlon, width)
        filtered = spectral_filter_grid(base, legendre, quadrature, doubling, cos_table, sin_table, filter_both)
        second = first + filtered.reshape(points, width)
        inner = rms_scale(second, norm_gains[2]).astype(jnp.bfloat16)
        hidden = lax.dot_general(inner, w_in, (((1,), (1,)), ((), ())), preferred_element_type=jnp.float32)
        hidden = jax.nn.gelu(hidden).astype(jnp.bfloat16)
        denoised = second + jnp.dot(hidden, w_down, preferred_element_type=jnp.float32)
        return (denoised + ratio * (state_frame - denoised)).astype(jnp.bfloat16)
    stepped = lax.map(one_frame, (scaled, mixed, state, ratios))
    return jnp.roll(stepped.reshape(frames, nlat, nlon, width), -1, axis=0)
```

```python
import jax
import jax.numpy as jnp
import ml_dtypes
import numpy as np
from jax import lax
from jax.experimental import pallas as pl
from jax.experimental.pallas import tpu as pltpu
from jax.sharding import PartitionSpec as P

F32, BF16 = jnp.float32, jnp.bfloat16
FRAMES, LATS, ROWS, NLON, NLAT, LMAX = 16, 32, 3, 192, 96, 96
POINTS, WIDTH, ATTN, FF = ROWS * NLON, 768, 384, 1536
ORDERS = LMAX // LATS
EPS = 1e-05
MIB = 1 << 20


def chunk_row(r):
    return r // 6, (r // 2) % 3, r % 2


def chunk_columns():
    listed = [(d,) + chunk_row(r) for d in range(LATS) for r in range(16)]
    for d in range(LATS):
        listed += [(d,) + chunk_row(16 + s % 2) if s < 6 else None for s in range(8)]
    return listed


def fourier_tables():
    forward = np.zeros((768, ROWS, NLON))
    inverse = np.zeros((768, ROWS, NLON))
    lon = np.arange(NLON)
    for at, entry in enumerate(chunk_columns()):
        if entry is None:
            continue
        owner, j, i, c = entry
        m = ORDERS * owner + i
        angle = 2 * np.pi * ((m * lon) % NLON) / NLON
        wave = np.cos(angle) if c == 0 else -np.sin(angle)
        forward[at, j] = wave
        inverse[at, j] = wave * (1.0 if m == 0 else 2.0)
    return (
        forward.reshape(768, POINTS).astype(ml_dtypes.bfloat16),
        np.ascontiguousarray(inverse.reshape(768, POINTS).T).astype(ml_dtypes.bfloat16),
    )


def placement_table():
    table = np.zeros((ORDERS, 2, NLAT, 768))
    for at, entry in enumerate(chunk_columns()):
        if entry is not None:
            source, j, i, c = entry
            table[i, c, ROWS * source + j, at] = 1.0
    return table.astype(ml_dtypes.bfloat16)


def legendre_tables():
    colatitude = np.pi * (np.arange(NLAT) + 0.5) / NLAT
    cosines = np.cos(colatitude)
    sine_rows = np.sin(colatitude)
    legendre = np.zeros((LMAX, LMAX, NLAT))
    for order_m in range(LMAX):
        counter = np.arange(1, order_m + 1)
        log_part = (
            0.5 * np.log((2 * order_m + 1) / (4 * np.pi))
            + 0.5 * np.sum(np.log((2 * counter - 1) / (2 * counter)))
            + order_m * np.log(sine_rows)
        )
        diagonal_value = (-1.0) ** order_m * np.exp(log_part)
        legendre[order_m, order_m] = diagonal_value
        if order_m + 1 < LMAX:
            legendre[order_m, order_m + 1] = cosines * np.sqrt(2 * order_m + 3) * diagonal_value
        for degree_l in range(order_m + 2, LMAX):
            factor_a = np.sqrt(
                (4.0 * degree_l * degree_l - 1) / (degree_l * degree_l - order_m * order_m)
            )
            factor_b = np.sqrt(
                ((degree_l - 1.0) ** 2 - order_m * order_m) / (4.0 * (degree_l - 1) ** 2 - 1)
            )
            legendre[order_m, degree_l] = factor_a * (
                cosines * legendre[order_m, degree_l - 1]
                - factor_b * legendre[order_m, degree_l - 2]
            )
    quadrature = sine_rows * (np.pi / NLAT) * (2 * np.pi / NLON)
    return legendre.astype(np.float32).astype(ml_dtypes.bfloat16), quadrature.astype(np.float32)


def swap4(first, second):
    low = lax.broadcasted_iota(jnp.int32, first.shape, 1) < 4
    rolled_first, rolled_second = pltpu.roll(first, 4, 1), pltpu.roll(second, 4, 1)
    return jnp.where(low, first, rolled_second), jnp.where(low, rolled_first, second)


def pairs(tiles):
    split = tiles.reshape(8, 2, 8, 128)
    return split[:, 0], split[:, 1]


def frame_scale(level):
    return lax.rsqrt(1.0 + level * level)


def row_scale(values):
    return lax.rsqrt(jnp.sum(values * values, axis=-1, keepdims=True) * (1.0 / WIDTH) + EPS)


def pack_window(window_ref, out_ref):
    for d in range(FRAMES):
        for block in range(2):
            for c in range(6):
                at = (block * 6 + c) * 16
                out_ref[d, at : at + 16, :] = window_ref[
                    32 * d + 16 * block : 32 * d + 16 * block + 16, 128 * c : 128 * c + 128
                ]
    for q in range(3):
        left = window_ref[512:576, 256 * q : 256 * q + 128].astype(F32).reshape(8, 8, 128)
        right = window_ref[512:576, 256 * q + 128 : 256 * q + 256].astype(F32).reshape(8, 8, 128)
        even, odd = swap4(left, right)
        at = 192 + 8 * q
        for i in range(8):
            out_ref[2 * i, at : at + 8, :] = even[i].astype(BF16)
            out_ref[2 * i + 1, at : at + 8, :] = odd[i].astype(BF16)


def attend(noise_ref, gains_ref, in_ref, w_ref, out_ref, x_ref, proj_ref):
    level = jnp.concatenate([jnp.full((1, 8, 128), noise_ref[f], F32) for f in range(FRAMES)], 0)
    scale = frame_scale(level)
    gain = [gains_ref[0:1, 128 * c : 128 * c + 128].reshape(1, 1, 128) for c in range(6)]
    for s in range(4):
        at = (s // 2) * 96 + 8 * (s % 2)
        parts = [in_ref[:, at + 16 * c : at + 16 * c + 8, :].astype(F32) * scale for c in range(6)]
        squares = sum(v * v for v in parts)
        r = lax.rsqrt(jnp.sum(squares, axis=-1, keepdims=True) * (1.0 / WIDTH) + EPS)
        for c in range(6):
            x_ref[128 * s : 128 * s + 128, 128 * c : 128 * c + 128] = (
                (parts[c] * r * gain[c]).reshape(128, 128).astype(BF16)
            )
    parts = [in_ref[:, 192 + 8 * q : 200 + 8 * q, :].astype(F32) * scale for q in range(3)]
    squares = sum(v * v for v in parts)
    total = jnp.broadcast_to(jnp.sum(squares, axis=-1, keepdims=True), squares.shape)
    r = lax.rsqrt((total + pltpu.roll(total, 4, 1)) * (1.0 / WIDTH) + EPS)
    low = lax.broadcasted_iota(jnp.int32, (1, 8, 128), 1) < 4
    for q in range(3):
        both = parts[q] * r * jnp.where(low, gain[2 * q], gain[2 * q + 1])
        left, right = swap4(*pairs(both))
        x_ref[512:576, 256 * q : 256 * q + 128] = left.reshape(64, 128).astype(BF16)
        x_ref[512:576, 256 * q + 128 : 256 * q + 256] = right.reshape(64, 128).astype(BF16)
    for b in range(3):
        proj_ref[:, ATTN * b : ATTN * (b + 1)] = jnp.dot(
            x_ref[...], w_ref[:, ATTN * b : ATTN * (b + 1)], preferred_element_type=F32
        ).astype(BF16)

    def mix(base, n):
        size = FRAMES * n
        row = lax.broadcasted_iota(jnp.int32, (1, size, size), 1)
        col = lax.broadcasted_iota(jnp.int32, (1, size, size), 2)
        kept = ((row & (n - 1)) == (col & (n - 1))) & (col // n <= row // n)
        lane = lax.broadcasted_iota(jnp.int32, (size, 128), 1) < 64
        one = jnp.where(lane, 1.0, 0.0).astype(BF16)
        other = jnp.where(lane, 0.0, 1.0).astype(BF16)
        results = []
        for h in range(3):
            q = proj_ref[base : base + size, 128 * h : 128 * h + 128]
            k = proj_ref[base : base + size, ATTN + 128 * h : ATTN + 128 * h + 128]
            v = proj_ref[base : base + size, 2 * ATTN + 128 * h : 2 * ATTN + 128 * h + 128]
            scores = lax.dot_general(
                jnp.concatenate([q * one, q * other], 0),
                k,
                (((1,), (1,)), ((), ())),
                preferred_element_type=F32,
            )
            scores = jnp.where(kept, scores.reshape(2, size, size) * 0.125, -1e30)
            expo = jnp.exp(scores - jnp.max(scores, axis=-1, keepdims=True))
            total = jnp.sum(expo, axis=-1, keepdims=True)
            weights = expo.reshape(2 * size, size).astype(BF16)
            mixed = jnp.dot(weights, v, preferred_element_type=F32).reshape(2, size, 128) / total
            results.append(jnp.where(lane, mixed[0], mixed[1]))
        return results

    for s in range(4):
        for h, mixed in enumerate(mix(128 * s, 8)):
            at = (s // 2) * 48 + 16 * h + 8 * (s % 2)
            mixed = mixed.reshape(FRAMES, 8, 128).astype(BF16)
            out_ref[0:15, at : at + 8, :] = mixed[1:16]
            out_ref[15:16, at : at + 8, :] = mixed[0:1]
    rest = [mixed.reshape(8, 8, 128) for mixed in mix(512, 4)]
    for at, (even, odd) in ((96, swap4(rest[0], rest[1])), (104, swap4(rest[2], rest[2]))):
        for i in range(8):
            out_ref[(2 * i - 1) % FRAMES, at : at + 8, :] = even[i].astype(BF16)
            out_ref[2 * i, at : at + 8, :] = odd[i].astype(BF16)


def put_chunks(values, out_ref):
    for c in range(6):
        block = values[:512, 128 * c : 128 * c + 128].reshape(LATS, 16, 128)
        out_ref[:, 16 * c : 16 * c + 16, :] = block.astype(BF16)
    slot = lax.broadcasted_iota(jnp.int32, (LATS, 8, 128), 1)
    for t in range(2):
        tile = None
        for q in range(3):
            at = 256 * q + 128 * t
            part = values[512:, at : at + 128].reshape(LATS, 8, 128)
            tile = part if tile is None else jnp.where(slot // 2 == q, part, tile)
        out_ref[:, 96 + 8 * t : 104 + 8 * t, :] = tile.astype(BF16)


def get_chunks(in_ref, rows_ref):
    for c in range(6):
        rows_ref[0:512, 128 * c : 128 * c + 128] = in_ref[:, 16 * c : 16 * c + 16, :].reshape(
            512, 128
        )
    slot = lax.broadcasted_iota(jnp.int32, (LATS, 8, 128), 1)
    for t in range(2):
        tile = in_ref[:, 96 + 8 * t : 104 + 8 * t, :].astype(F32)
        for q in range(3):
            at = 256 * q + 128 * t
            rows_ref[512:768, at : at + 128] = (
                jnp.where(slot // 2 == q, tile, 0.0).reshape(256, 128).astype(BF16)
            )


def to_spectra(
    where_ref, noise_ref, quad_ref, gains_ref, mixed_ref, window_ref, w_ref, table_ref,
    first_ref, out_ref, mixed_rows, base_rows,
):
    for block in range(2):
        for h in range(3):
            at = (block * 3 + h) * 16
            for d in range(FRAMES):
                mixed_rows[
                    32 * d + 16 * block : 32 * d + 16 * block + 16, 128 * h : 128 * h + 128
                ] = mixed_ref[d, at : at + 16, :]
    left, right = swap4(*pairs(mixed_ref[:, 96:104, :].astype(F32)))
    last, _ = swap4(*pairs(mixed_ref[:, 104:112, :].astype(F32)))
    for h, tile in enumerate((left, right, last)):
        mixed_rows[512:576, 128 * h : 128 * h + 128] = tile.reshape(64, 128).astype(BF16)
    scale = frame_scale(jnp.full((1, 1), noise_ref[where_ref[0]], F32))
    gain = gains_ref[1:2, :]
    for j in range(ROWS):
        rows = slice(NLON * j, NLON * (j + 1))
        first = window_ref[rows, :].astype(F32) * scale + jnp.dot(
            mixed_rows[rows, :], w_ref[...], preferred_element_type=F32
        )
        first_ref[rows, :] = first
        weight = quad_ref[ROWS * where_ref[1] + j]
        base_rows[rows, :] = (first * (row_scale(first) * weight) * gain).astype(BF16)
    put_chunks(jnp.dot(table_ref[...], base_rows[...], preferred_element_type=F32), out_ref)


def filter_orders(in_ref, down_ref, up_ref, filter_ref, out_ref, rows_ref, coeffs_ref):
    get_chunks(in_ref, rows_ref)
    factor = filter_ref[...].astype(F32)
    coeffs = jnp.dot(down_ref[...], rows_ref[...], preferred_element_type=F32)
    for b in range(2 * ORDERS):
        rows = slice(LMAX * b, LMAX * (b + 1))
        coeffs_ref[rows, :] = (coeffs[rows] * factor).astype(BF16)
    put_chunks(jnp.dot(up_ref[...], coeffs_ref[...], preferred_element_type=F32), out_ref)


def gelu(x):
    return 0.5 * x * (1.0 + jnp.tanh(np.float32(np.sqrt(2 / np.pi)) * (x + 0.044715 * (x * x * x))))


def feed_forward(
    where_ref, keep_ref, gains_ref, in_ref, table_ref, first_ref, window_ref, w_ref,
    out_ref, rows_ref, inner_ref, total_ref,
):
    get_chunks(in_ref, rows_ref)
    gain = gains_ref[2:3, :]
    second = first_ref[...] + jnp.dot(table_ref[...], rows_ref[...], preferred_element_type=F32)
    total_ref[...] = second
    inner_ref[...] = (second * row_scale(second) * gain).astype(BF16)
    for b in range(4):
        w_in = w_ref[4 * b : 4 * b + 4, 0:96, :].reshape(384, WIDTH)
        w_down = w_ref[4 * b : 4 * b + 4, 96:192, :].reshape(384, WIDTH)
        raised = lax.dot_general(
            inner_ref[...], w_in, (((1,), (1,)), ((), ())), preferred_element_type=F32
        )
        total_ref[...] += jnp.dot(
            gelu(raised).astype(BF16), w_down, preferred_element_type=F32
        )
    frame = where_ref[0]
    ratio = jnp.where(frame == 0, 0.0, keep_ref[frame])
    denoised = total_ref[...]
    out_ref[...] = (denoised + ratio * (window_ref[...].astype(F32) - denoised)).astype(BF16)


def call(kernel, out_shape, specs, scratch, args, flops=0, moved=0, limit=40):
    spaces = {"v": pltpu.VMEM, "s": pltpu.SMEM}
    outs = out_shape if isinstance(out_shape, list) else [out_shape]
    result = pl.pallas_call(
        kernel,
        out_shape=out_shape,
        in_specs=[pl.BlockSpec(memory_space=spaces[kind]) for kind in specs],
        out_specs=jax.tree.map(lambda _: pl.BlockSpec(memory_space=pltpu.VMEM), out_shape),
        scratch_shapes=[pltpu.VMEM(shape, dtype) for shape, dtype in scratch],
        compiler_params=pltpu.CompilerParams(vmem_limit_bytes=limit * MIB),
        cost_estimate=pl.CostEstimate(
            flops=flops,
            bytes_accessed=sum(a.size * a.dtype.itemsize for a in list(args) + outs),
            transcendentals=0,
        ),
    )(*args)
    return result


def exchange(chunks, axis):
    return lax.all_to_all(chunks, axis, split_axis=0, concat_axis=0, tiled=True)


def per_device(
    window, noise_level, keep_ratio, norm_gains, w_qkv, w_out, spectral_filter, w_in, w_down
):
    lead, lat = lax.axis_index("lead"), lax.axis_index("lat")
    frame = (lead + 1) % FRAMES
    here = jnp.stack([frame, lat]).astype(jnp.int32)
    forward, inverse = (jnp.asarray(table) for table in fourier_tables())
    legendre, quadrature = (jnp.asarray(table) for table in legendre_tables())
    placement = jnp.asarray(placement_table())
    shape = jax.ShapeDtypeStruct

    state = window.reshape(POINTS, WIDTH)
    packed = call(pack_window, shape((FRAMES, 216, 128), BF16), "v", [], [state])
    ahead = lax.ppermute(
        state, "lead", [(source, (source - 1) % FRAMES) for source in range(FRAMES)]
    )
    packed, legendre = lax.optimization_barrier((packed, legendre))
    local = lax.dynamic_slice_in_dim(legendre, ORDERS * lat, ORDERS, 0)
    down = jnp.einsum("ilj,icjn->icln", local, placement, preferred_element_type=F32)
    down = down.astype(BF16).reshape(2 * ORDERS * LMAX, 768)
    up = down.T

    mixed = call(
        attend,
        shape((FRAMES, 112, 128), BF16),
        "svvv",
        [((POINTS, WIDTH), BF16), ((POINTS, 3 * ATTN), BF16)],
        [noise_level, norm_gains, exchange(packed, "lead"), w_qkv],
        flops=2 * POINTS * WIDTH * 3 * ATTN,
    )
    mixed = exchange(mixed, "lead")
    weights = jnp.concatenate([w_in, w_down], 0)
    mixed, weights = lax.optimization_barrier((mixed, weights))
    weights = lax.all_gather(weights, "lead", axis=0, tiled=False)
    first, spectra = call(
        to_spectra,
        [shape((POINTS, WIDTH), F32), shape((LATS, 112, 128), BF16)],
        "sssvvvvv",
        [((POINTS, ATTN), BF16), ((POINTS, WIDTH), BF16)],
        [here, noise_level, quadrature, norm_gains, mixed, ahead, w_out, forward],
        flops=2 * POINTS * WIDTH * (ATTN + 768),
    )
    back = call(
        filter_orders,
        shape((LATS, 112, 128), BF16),
        "vvvv",
        [((768, WIDTH), BF16), ((2 * ORDERS * LMAX, WIDTH), BF16)],
        [exchange(spectra, "lat"), down, up, spectral_filter],
        flops=4 * POINTS * WIDTH * 768,
    )
    stepped = call(
        feed_forward,
        shape((POINTS, WIDTH), BF16),
        "ssvvvvvv",
        [((768, WIDTH), BF16), ((POINTS, WIDTH), BF16), ((POINTS, WIDTH), F32)],
        [here, keep_ratio, norm_gains, exchange(back, "lat"), inverse, first, ahead, weights],
        flops=2 * POINTS * WIDTH * (2 * FF + 768),
    )
    return stepped.reshape(1, ROWS, NLON, WIDTH)


def solution(mesh):
    return jax.shard_map(
        per_device,
        mesh=mesh,
        in_specs=(
            P("lead", "lat", None, None),
            P(),
            P(),
            P(),
            P(),
            P(),
            P(),
            P("lead", None),
            P("lead", None),
        ),
        out_specs=P("lead", "lat", None, None),
        check_vma=False,
    )
```

```python
import jax
import jax.numpy as jnp
import ml_dtypes
import numpy as np
from jax import lax
from jax.experimental import pallas as pl
from jax.experimental.pallas import tpu as pltpu
from jax.sharding import PartitionSpec as P

F32, BF16 = jnp.float32, jnp.bfloat16
FRAMES, LATS, ROWS, NLON, NLAT, LMAX = 16, 32, 3, 192, 96, 96
POINTS, WIDTH, ATTN, FF = ROWS * NLON, 768, 384, 1536
ORDERS = LMAX // LATS
EPS = 1e-05
MIB = 1 << 20
LIMITS = (60, 51, 52, 45, 51)


def chunk_row(r):
    return r // 6, (r // 2) % 3, r % 2


def chunk_columns():
    listed = [(d,) + chunk_row(r) for d in range(LATS) for r in range(16)]
    for d in range(LATS):
        listed += [(d,) + chunk_row(16 + s % 2) if s < 6 else None for s in range(8)]
    return listed


def fourier_tables():
    forward = np.zeros((768, ROWS, NLON))
    inverse = np.zeros((768, ROWS, NLON))
    lon = np.arange(NLON)
    for at, entry in enumerate(chunk_columns()):
        if entry is None:
            continue
        owner, j, i, c = entry
        m = ORDERS * owner + i
        angle = 2 * np.pi * ((m * lon) % NLON) / NLON
        wave = np.cos(angle) if c == 0 else -np.sin(angle)
        forward[at, j] = wave
        inverse[at, j] = wave * (1.0 if m == 0 else 2.0)
    tables = np.zeros((2, 768, 768))
    tables[0, :, :POINTS] = forward.reshape(768, POINTS)
    tables[1, :POINTS] = inverse.reshape(768, POINTS).T
    return tables.astype(ml_dtypes.bfloat16)


def placement_table():
    table = np.zeros((ORDERS, 2, NLAT, 768))
    for at, entry in enumerate(chunk_columns()):
        if entry is not None:
            source, j, i, c = entry
            table[i, c, ROWS * source + j, at] = 1.0
    return table.astype(ml_dtypes.bfloat16)


def legendre_tables():
    colatitude = np.pi * (np.arange(NLAT) + 0.5) / NLAT
    cosines = np.cos(colatitude)
    sine_rows = np.sin(colatitude)
    legendre = np.zeros((LMAX, LMAX, NLAT))
    for order_m in range(LMAX):
        counter = np.arange(1, order_m + 1)
        log_part = (
            0.5 * np.log((2 * order_m + 1) / (4 * np.pi))
            + 0.5 * np.sum(np.log((2 * counter - 1) / (2 * counter)))
            + order_m * np.log(sine_rows)
        )
        diagonal_value = (-1.0) ** order_m * np.exp(log_part)
        legendre[order_m, order_m] = diagonal_value
        if order_m + 1 < LMAX:
            legendre[order_m, order_m + 1] = cosines * np.sqrt(2 * order_m + 3) * diagonal_value
        for degree_l in range(order_m + 2, LMAX):
            factor_a = np.sqrt(
                (4.0 * degree_l * degree_l - 1) / (degree_l * degree_l - order_m * order_m)
            )
            factor_b = np.sqrt(
                ((degree_l - 1.0) ** 2 - order_m * order_m) / (4.0 * (degree_l - 1) ** 2 - 1)
            )
            legendre[order_m, degree_l] = factor_a * (
                cosines * legendre[order_m, degree_l - 1]
                - factor_b * legendre[order_m, degree_l - 2]
            )
    quadrature = sine_rows * (np.pi / NLAT) * (2 * np.pi / NLON)
    return np.stack([legendre * quadrature, legendre]).astype(ml_dtypes.bfloat16)


def swap4(first, second):
    low = lax.broadcasted_iota(jnp.int32, first.shape, 1) < 4
    rolled_first, rolled_second = pltpu.roll(first, 4, 1), pltpu.roll(second, 4, 1)
    return jnp.where(low, first, rolled_second), jnp.where(low, rolled_first, second)


def pairs(tiles):
    split = tiles.reshape(8, 2, 8, 128)
    return split[:, 0], split[:, 1]


def fetch(source, target, sem):
    copy = pltpu.make_async_copy(source, target, sem)
    copy.start()
    return copy


def frame_scale(level):
    return lax.rsqrt(1.0 + level * level)


def row_scale(values):
    return lax.rsqrt(jnp.sum(values * values, axis=-1, keepdims=True) * (1.0 / WIDTH) + EPS)


def pack_window(window_any, out_any, last_ref, packed_ref, sems):
    last = fetch(window_any.at[16:18], last_ref, sems.at[0])
    copies = [
        fetch(
            window_any.at[0:16, :, :, ATTN * h : ATTN * h + ATTN],
            out_any.at[:, 4 * h : 4 * h + 4],
            sems.at[1 + h],
        )
        for h in range(2)
    ]
    last.wait()
    for c in range(3):
        left = last_ref[:, :, :, 128 * c : 128 * c + 128].astype(F32).reshape(8, 8, 128)
        right = last_ref[:, :, :, ATTN + 128 * c : ATTN + 128 * c + 128].astype(F32)
        even, odd = swap4(left, right.reshape(8, 8, 128))
        for i in range(8):
            packed_ref[2 * i, :, 128 * c : 128 * c + 128] = even[i].astype(BF16)
            packed_ref[2 * i + 1, :, 128 * c : 128 * c + 128] = odd[i].astype(BF16)
    copies.append(fetch(packed_ref, out_any.at[:, 8], sems.at[3]))
    for copy in copies:
        copy.wait()


def attend(noise_ref, gains_ref, in_ref, w_ref, out_ref, x_ref, proj_ref):
    level = jnp.concatenate([jnp.full((1, 8, 128), noise_ref[f], F32) for f in range(FRAMES)], 0)
    scale = frame_scale(level)
    gain = [gains_ref[0:1, 128 * c : 128 * c + 128].reshape(1, 1, 128) for c in range(6)]
    for s in range(4):
        parts = [
            in_ref[:, 4 * (c // 3) + s, :, 128 * (c % 3) : 128 * (c % 3) + 128].astype(F32) * scale
            for c in range(6)
        ]
        squares = sum(v * v for v in parts)
        r = lax.rsqrt(jnp.sum(squares, axis=-1, keepdims=True) * (1.0 / WIDTH) + EPS)
        for c in range(6):
            x_ref[128 * s : 128 * s + 128, 128 * c : 128 * c + 128] = (
                (parts[c] * r * gain[c]).reshape(128, 128).astype(BF16)
            )
    parts = [in_ref[:, 8, :, 128 * c : 128 * c + 128].astype(F32) * scale for c in range(3)]
    squares = sum(v * v for v in parts)
    total = jnp.broadcast_to(jnp.sum(squares, axis=-1, keepdims=True), squares.shape)
    r = lax.rsqrt((total + pltpu.roll(total, 4, 1)) * (1.0 / WIDTH) + EPS)
    low = lax.broadcasted_iota(jnp.int32, (1, 8, 128), 1) < 4
    for c in range(3):
        both = parts[c] * r * jnp.where(low, gain[c], gain[c + 3])
        left, right = swap4(*pairs(both))
        x_ref[512:576, 128 * c : 128 * c + 128] = left.reshape(64, 128).astype(BF16)
        x_ref[512:576, ATTN + 128 * c : ATTN + 128 * c + 128] = right.reshape(64, 128).astype(BF16)
    for b in range(3):
        proj_ref[:, ATTN * b : ATTN * (b + 1)] = jnp.dot(
            x_ref[...], w_ref[:, ATTN * b : ATTN * (b + 1)], preferred_element_type=F32
        ).astype(BF16)

    def mix(base, n):
        size = FRAMES * n
        row = lax.broadcasted_iota(jnp.int32, (1, size, size), 1)
        col = lax.broadcasted_iota(jnp.int32, (1, size, size), 2)
        kept = ((row & (n - 1)) == (col & (n - 1))) & (col // n <= row // n)
        lane = lax.broadcasted_iota(jnp.int32, (size, 128), 1) < 64
        one = jnp.where(lane, 1.0, 0.0).astype(BF16)
        other = jnp.where(lane, 0.0, 1.0).astype(BF16)
        results = []
        for h in range(3):
            q = proj_ref[base : base + size, 128 * h : 128 * h + 128]
            k = proj_ref[base : base + size, ATTN + 128 * h : ATTN + 128 * h + 128]
            v = proj_ref[base : base + size, 2 * ATTN + 128 * h : 2 * ATTN + 128 * h + 128]
            scores = lax.dot_general(
                jnp.concatenate([q * one, q * other], 0),
                k,
                (((1,), (1,)), ((), ())),
                preferred_element_type=F32,
            )
            scores = jnp.where(kept, scores.reshape(2, size, size) * 0.125, -1e30)
            expo = jnp.exp(scores - jnp.max(scores, axis=-1, keepdims=True))
            total = jnp.sum(expo, axis=-1, keepdims=True)
            weights = expo.reshape(2 * size, size).astype(BF16)
            mixed = jnp.dot(weights, v, preferred_element_type=F32).reshape(2, size, 128) / total
            results.append(jnp.where(lane, mixed[0], mixed[1]))
        return results

    for s in range(4):
        for h, mixed in enumerate(mix(128 * s, 8)):
            at = (s // 2) * 48 + 16 * h + 8 * (s % 2)
            mixed = mixed.reshape(FRAMES, 8, 128).astype(BF16)
            out_ref[0:15, at : at + 8, :] = mixed[1:16]
            out_ref[15:16, at : at + 8, :] = mixed[0:1]
    rest = [mixed.reshape(8, 8, 128) for mixed in mix(512, 4)]
    for at, (even, odd) in ((96, swap4(rest[0], rest[1])), (104, swap4(rest[2], rest[2]))):
        for i in range(8):
            out_ref[(2 * i - 1) % FRAMES, at : at + 8, :] = even[i].astype(BF16)
            out_ref[2 * i, at : at + 8, :] = odd[i].astype(BF16)


def put_chunks(values, out_ref):
    for c in range(6):
        block = values[:512, 128 * c : 128 * c + 128].reshape(LATS, 16, 128)
        out_ref[:, 16 * c : 16 * c + 16, :] = block.astype(BF16)
    slot = lax.broadcasted_iota(jnp.int32, (LATS, 8, 128), 1)
    for t in range(2):
        tile = None
        for q in range(3):
            at = 256 * q + 128 * t
            part = values[512:, at : at + 128].reshape(LATS, 8, 128)
            tile = part if tile is None else jnp.where(slot // 2 == q, part, tile)
        out_ref[:, 96 + 8 * t : 104 + 8 * t, :] = tile.astype(BF16)


def get_chunks(in_ref, rows_ref):
    for c in range(6):
        rows_ref[0:512, 128 * c : 128 * c + 128] = in_ref[:, 16 * c : 16 * c + 16, :].reshape(
            512, 128
        )
    slot = lax.broadcasted_iota(jnp.int32, (LATS, 8, 128), 1)
    for t in range(2):
        tile = in_ref[:, 96 + 8 * t : 104 + 8 * t, :].astype(F32)
        for q in range(3):
            at = 256 * q + 128 * t
            rows_ref[512:768, at : at + 128] = (
                jnp.where(slot // 2 == q, tile, 0.0).reshape(256, 128).astype(BF16)
            )


def to_spectra(
    frame_ref, noise_ref, gains_ref, mixed_ref, window_any, w_any, tables_any,
    first_any, out_ref, mixed_rows, base_rows, first_ref, window_ref, w_ref, table_ref, sems,
):
    w_copy = fetch(w_any, w_ref, sems.at[0])
    window_copy = fetch(window_any, window_ref, sems.at[1])
    table_copy = fetch(tables_any.at[0, :, 0:640], table_ref, sems.at[2])
    for block in range(2):
        for h in range(3):
            at = (block * 3 + h) * 16
            for d in range(FRAMES):
                mixed_rows[
                    32 * d + 16 * block : 32 * d + 16 * block + 16, 128 * h : 128 * h + 128
                ] = mixed_ref[d, at : at + 16, :]
    left, right = swap4(*pairs(mixed_ref[:, 96:104, :].astype(F32)))
    last, _ = swap4(*pairs(mixed_ref[:, 104:112, :].astype(F32)))
    for h, tile in enumerate((left, right, last)):
        mixed_rows[512:576, 128 * h : 128 * h + 128] = tile.reshape(64, 128).astype(BF16)
    scale = frame_scale(jnp.full((1, 1), noise_ref[frame_ref[0]], F32))
    gain = gains_ref[1:2, :]
    w_copy.wait()
    window_copy.wait()
    first = window_ref[...].astype(F32) * scale + jnp.dot(
        mixed_rows[...], w_ref[...], preferred_element_type=F32
    )
    first_ref[...] = first
    first_copy = fetch(first_ref, first_any, sems.at[3])
    base_rows[0:POINTS, :] = (first * row_scale(first) * gain).astype(BF16)
    base_rows[POINTS:640, :] = jnp.zeros((640 - POINTS, WIDTH), BF16)
    table_copy.wait()
    put_chunks(jnp.dot(table_ref[...], base_rows[...], preferred_element_type=F32), out_ref)
    first_copy.wait()


def filter_orders(in_ref, down_ref, up_ref, filter_ref, out_ref, rows_ref, coeffs_ref):
    get_chunks(in_ref, rows_ref)
    factor = filter_ref[...].astype(F32)
    coeffs = jnp.dot(down_ref[...], rows_ref[...], preferred_element_type=F32)
    for b in range(2 * ORDERS):
        rows = slice(LMAX * b, LMAX * (b + 1))
        coeffs_ref[rows, :] = (coeffs[rows] * factor).astype(BF16)
    put_chunks(jnp.dot(up_ref[...], coeffs_ref[...], preferred_element_type=F32), out_ref)


def gelu(x):
    return 0.5 * x * (1.0 + jnp.tanh(np.float32(np.sqrt(2 / np.pi)) * (x + 0.044715 * (x * x * x))))


def feed_forward(
    frame_ref, keep_ref, gains_ref, in_ref, tables_any, first_any, window_any, weights_any,
    out_any, rows_ref, inner_ref, hidden_ref, out_ref, table_ref, first_ref, window_ref,
    w_in_ref, w_down_ref, sems,
):
    table_copy = fetch(tables_any.at[1, 0:POINTS], table_ref, sems.at[0])
    first_copy = fetch(first_any, first_ref, sems.at[1])
    get_chunks(in_ref, rows_ref)
    in_copy = fetch(weights_any.at[:, 0:96, :], w_in_ref, sems.at[2])
    gain = gains_ref[2:3, :]
    table_copy.wait()
    first_copy.wait()
    down_copy = fetch(weights_any.at[:, 96:192, :], w_down_ref, sems.at[3])
    window_copy = fetch(window_any, window_ref, sems.at[4])
    second = first_ref[...] + jnp.dot(table_ref[...], rows_ref[...], preferred_element_type=F32)
    first_ref[...] = second
    inner_ref[...] = (second * row_scale(second) * gain).astype(BF16)
    in_copy.wait()
    for b in range(2):
        units = slice(8 * b, 8 * b + 8)
        raised = lax.dot_general(
            inner_ref[...],
            w_in_ref[units].reshape(FF // 2, WIDTH),
            (((1,), (1,)), ((), ())),
            preferred_element_type=F32,
        )
        hidden_ref[:, FF // 2 * b : FF // 2 * (b + 1)] = gelu(raised).astype(BF16)
    frame = frame_ref[0]
    ratio = jnp.where(frame == 0, 0.0, keep_ref[frame])
    down_copy.wait()
    window_copy.wait()
    w_down = w_down_ref[...].reshape(FF, WIDTH)
    copies = []
    for j in range(2):
        rows = slice(POINTS // 2 * j, POINTS // 2 * (j + 1))
        denoised = first_ref[rows, :] + jnp.dot(
            hidden_ref[rows, :], w_down, preferred_element_type=F32
        )
        state = window_ref[rows, :].astype(F32)
        out_ref[rows, :] = (denoised + ratio * (state - denoised)).astype(BF16)
        copies.append(fetch(out_ref.at[rows], out_any.at[rows], sems.at[5 + j]))
    for copy in copies:
        copy.wait()


SPACES = {"v": pltpu.VMEM, "s": pltpu.SMEM, "h": pltpu.HBM}


def call(kernel, outs, kinds, scratch, args, flops, limit):
    specs = [pl.BlockSpec(memory_space=SPACES[kind]) for kind in kinds]
    return pl.pallas_call(
        kernel,
        out_shape=outs,
        in_specs=specs[: len(args)],
        out_specs=specs[len(args) :],
        scratch_shapes=[
            pltpu.VMEM(*entry) if isinstance(entry, tuple) else pltpu.SemaphoreType.DMA((entry,))
            for entry in scratch
        ],
        compiler_params=pltpu.CompilerParams(vmem_limit_bytes=int(limit * MIB)),
        cost_estimate=pl.CostEstimate(
            flops=flops,
            bytes_accessed=sum(a.size * a.dtype.itemsize for a in list(args) + outs),
            transcendentals=0,
        ),
    )(*args)


def exchange(chunks, axis):
    return lax.all_to_all(chunks, axis, split_axis=0, concat_axis=0, tiled=True)


def per_device(
    window, noise_level, keep_ratio, norm_gains, w_qkv, w_out, spectral_filter, w_in, w_down
):
    lead, lat = lax.axis_index("lead"), lax.axis_index("lat")
    frame = ((lead + 1) & (FRAMES - 1)).astype(jnp.int32).reshape(1)
    tables = jnp.asarray(fourier_tables())
    legendre = jnp.asarray(legendre_tables())
    placement = jnp.asarray(placement_table())
    shape = jax.ShapeDtypeStruct

    state = window.reshape(POINTS, WIDTH)
    (packed,) = call(
        pack_window,
        [shape((FRAMES, 9, 8, ATTN), BF16)],
        "hh",
        [((2, 4, 8, WIDTH), BF16), ((FRAMES, 8, ATTN), BF16), 4],
        [window.reshape(18, 4, 8, WIDTH)],
        0,
        LIMITS[0],
    )
    ahead = lax.ppermute(
        state, "lead", [(source, (source - 1) % FRAMES) for source in range(FRAMES)]
    )
    packed, legendre = lax.optimization_barrier((packed, legendre))
    local = lax.dynamic_slice_in_dim(legendre, ORDERS * lat, ORDERS, 1)
    down = jnp.einsum("ilj,icjn->icln", local[0], placement, preferred_element_type=F32)
    down = down.astype(BF16).reshape(2 * ORDERS * LMAX, 768)
    up = jnp.einsum("ilj,icjn->nicl", local[1], placement, preferred_element_type=F32)
    up = up.astype(BF16).reshape(768, 2 * ORDERS * LMAX)

    (mixed,) = call(
        attend,
        [shape((FRAMES, 112, 128), BF16)],
        "svvvv",
        [((POINTS, WIDTH), BF16), ((POINTS, 3 * ATTN), BF16)],
        [noise_level, norm_gains, exchange(packed, "lead"), w_qkv],
        2 * POINTS * WIDTH * 3 * ATTN,
        LIMITS[1],
    )
    mixed, ahead = lax.optimization_barrier((mixed, ahead))
    mixed = exchange(mixed, "lead")
    weights = jnp.concatenate([w_in, w_down], 0)
    mixed, weights = lax.optimization_barrier((mixed, weights))
    weights = lax.all_gather(weights, "lead", axis=0, tiled=False)
    first, spectra = call(
        to_spectra,
        [shape((POINTS, WIDTH), F32), shape((LATS, 112, 128), BF16)],
        "ssvvhhhhv",
        [
            ((POINTS, ATTN), BF16),
            ((640, WIDTH), BF16),
            ((POINTS, WIDTH), F32),
            ((POINTS, WIDTH), BF16),
            ((ATTN, WIDTH), BF16),
            ((768, 640), BF16),
            4,
        ],
        [frame, noise_level, norm_gains, mixed, ahead, w_out, tables],
        2 * POINTS * WIDTH * (ATTN + 768),
        LIMITS[2],
    )
    (back,) = call(
        filter_orders,
        [shape((LATS, 112, 128), BF16)],
        "vvvvv",
        [((768, WIDTH), BF16), ((2 * ORDERS * LMAX, WIDTH), BF16)],
        [exchange(spectra, "lat"), down, up, spectral_filter],
        4 * POINTS * WIDTH * 768,
        LIMITS[3],
    )
    (stepped,) = call(
        feed_forward,
        [shape((POINTS, WIDTH), BF16)],
        "ssvvhhhhh",
        [
            ((768, WIDTH), BF16),
            ((POINTS, WIDTH), BF16),
            ((POINTS, FF), BF16),
            ((POINTS, WIDTH), BF16),
            ((POINTS, 768), BF16),
            ((POINTS, WIDTH), F32),
            ((POINTS, WIDTH), BF16),
            ((FRAMES, 96, WIDTH), BF16),
            ((FRAMES, 96, WIDTH), BF16),
            7,
        ],
        [frame, keep_ratio, norm_gains, exchange(back, "lat"), tables, first, ahead, weights],
        2 * POINTS * WIDTH * (2 * FF + 768),
        LIMITS[4],
    )
    return stepped.reshape(1, ROWS, NLON, WIDTH)


def solution(mesh):
    return jax.shard_map(
        per_device,
        mesh=mesh,
        in_specs=(
            P("lead", "lat", None, None),
            P(),
            P(),
            P(),
            P(),
            P(),
            P(),
            P("lead", None),
            P("lead", None),
        ),
        out_specs=P("lead", "lat", None, None),
        check_vma=False,
    )
```

```python
import jax
import jax.numpy as jnp
import ml_dtypes
import numpy as np
from jax import lax
from jax.experimental import pallas as pl
from jax.experimental.pallas import tpu as pltpu
from jax.sharding import PartitionSpec as P

F32, BF16 = jnp.float32, jnp.bfloat16
FRAMES, LATS, ROWS, NLON, NLAT, LMAX = 16, 32, 3, 192, 96, 96
POINTS, WIDTH, ATTN, FF = ROWS * NLON, 768, 384, 1536
ORDERS = LMAX // LATS
EPS = 1e-05
SHARDS = 9
BLOCKS = tuple((b, slice(ATTN * b, ATTN * (b + 1))) for b in range(3))
MIB = 1 << 20
LIMITS = (60, 51, 52, 16, 49)


def chunk_row(r):
    return r // 6, (r // 2) % 3, r % 2


def chunk_columns():
    listed = [(d,) + chunk_row(r) for d in range(LATS) for r in range(16)]
    for d in range(LATS):
        listed += [(d,) + chunk_row(16 + s % 2) if s < 6 else None for s in range(8)]
    return listed


def fourier_tables():
    forward = np.zeros((768, ROWS, NLON))
    inverse = np.zeros((768, ROWS, NLON))
    lon = np.arange(NLON)
    for at, entry in enumerate(chunk_columns()):
        if entry is None:
            continue
        owner, j, i, c = entry
        m = ORDERS * owner + i
        angle = 2 * np.pi * ((m * lon) % NLON) / NLON
        wave = np.cos(angle) if c == 0 else -np.sin(angle)
        forward[at, j] = wave
        inverse[at, j] = wave * (1.0 if m == 0 else 2.0)
    tables = np.zeros((2, 768, 768))
    tables[0, :, :POINTS] = forward.reshape(768, POINTS)
    tables[1, :POINTS] = inverse.reshape(768, POINTS).T
    return tables.astype(ml_dtypes.bfloat16)


def placement_table():
    table = np.zeros((ORDERS, 2, NLAT, 768))
    for at, entry in enumerate(chunk_columns()):
        if entry is not None:
            source, j, i, c = entry
            table[i, c, ROWS * source + j, at] = 1.0
    return table.astype(ml_dtypes.bfloat16)


def legendre_tables():
    colatitude = np.pi * (np.arange(NLAT) + 0.5) / NLAT
    cosines = np.cos(colatitude)
    sine_rows = np.sin(colatitude)
    legendre = np.zeros((LMAX, LMAX, NLAT))
    for order_m in range(LMAX):
        counter = np.arange(1, order_m + 1)
        log_part = (
            0.5 * np.log((2 * order_m + 1) / (4 * np.pi))
            + 0.5 * np.sum(np.log((2 * counter - 1) / (2 * counter)))
            + order_m * np.log(sine_rows)
        )
        diagonal_value = (-1.0) ** order_m * np.exp(log_part)
        legendre[order_m, order_m] = diagonal_value
        if order_m + 1 < LMAX:
            legendre[order_m, order_m + 1] = cosines * np.sqrt(2 * order_m + 3) * diagonal_value
        for degree_l in range(order_m + 2, LMAX):
            factor_a = np.sqrt(
                (4.0 * degree_l * degree_l - 1) / (degree_l * degree_l - order_m * order_m)
            )
            factor_b = np.sqrt(
                ((degree_l - 1.0) ** 2 - order_m * order_m) / (4.0 * (degree_l - 1) ** 2 - 1)
            )
            legendre[order_m, degree_l] = factor_a * (
                cosines * legendre[order_m, degree_l - 1]
                - factor_b * legendre[order_m, degree_l - 2]
            )
    quadrature = sine_rows * (np.pi / NLAT) * (2 * np.pi / NLON)
    return np.stack([legendre * quadrature, legendre]).astype(ml_dtypes.bfloat16)


def swap4(first, second):
    low = lax.broadcasted_iota(jnp.int32, first.shape, 1) < 4
    rolled_first, rolled_second = pltpu.roll(first, 4, 1), pltpu.roll(second, 4, 1)
    return jnp.where(low, first, rolled_second), jnp.where(low, rolled_first, second)


def pairs(tiles):
    split = tiles.reshape(8, 2, 8, 128)
    return split[:, 0], split[:, 1]


def fetch(source, target, sem):
    copy = pltpu.make_async_copy(source, target, sem)
    copy.start()
    return copy


def row_scale(values):
    return lax.rsqrt(jnp.sum(values * values, axis=-1, keepdims=True) * (1.0 / WIDTH) + EPS)


def pack_window(noise_ref, keep_ref, gains_ref, window_ref, out_ref, params_ref):
    for f in range(FRAMES):
        level = jnp.full((8, 128), noise_ref[f], F32)
        params_ref[f] = lax.rsqrt(1.0 + level * level)
        params_ref[FRAMES + f] = jnp.full((8, 128), 0.0 if f == 0 else keep_ref[f], F32)
    for norm in range(3):
        for c in range(6):
            params_ref[2 * FRAMES + norm, c : c + 1, :] = gains_ref[
                norm : norm + 1, 128 * c : 128 * c + 128
            ]
    for h in range(2):
        out_ref[:, 4 * h : 4 * h + 4] = window_ref[0:16, :, :, ATTN * h : ATTN * h + ATTN]
    for c in range(3):
        left = window_ref[16:18, :, :, 128 * c : 128 * c + 128].astype(F32).reshape(8, 8, 128)
        right = window_ref[16:18, :, :, ATTN + 128 * c : ATTN + 128 * c + 128].astype(F32)
        even, odd = swap4(left, right.reshape(8, 8, 128))
        for i in range(8):
            out_ref[2 * i, 8, :, 128 * c : 128 * c + 128] = even[i].astype(BF16)
            out_ref[2 * i + 1, 8, :, 128 * c : 128 * c + 128] = odd[i].astype(BF16)


def gain_row(params_ref, norm):
    return jnp.concatenate([params_ref[2 * FRAMES + norm, c : c + 1, :] for c in range(6)], 1)


def attend(params_ref, in_ref, w_any, out_ref, x_ref, proj_ref, w_ref, sems):
    w_copies = [fetch(w_any.at[:, cols], w_ref.at[:, cols], sems.at[b]) for b, cols in BLOCKS]
    scale = params_ref[0:FRAMES]
    gain = [params_ref[2 * FRAMES, c : c + 1, :].reshape(1, 1, 128) for c in range(6)]
    for s in range(4):
        parts = [
            in_ref[:, 4 * (c // 3) + s, :, 128 * (c % 3) : 128 * (c % 3) + 128].astype(F32) * scale
            for c in range(6)
        ]
        squares = sum(v * v for v in parts)
        r = lax.rsqrt(jnp.sum(squares, axis=-1, keepdims=True) * (1.0 / WIDTH) + EPS)
        for c in range(6):
            x_ref[128 * s : 128 * s + 128, 128 * c : 128 * c + 128] = (
                (parts[c] * r * gain[c]).reshape(128, 128).astype(BF16)
            )
    parts = [in_ref[:, 8, :, 128 * c : 128 * c + 128].astype(F32) * scale for c in range(3)]
    squares = sum(v * v for v in parts)
    total = jnp.broadcast_to(jnp.sum(squares, axis=-1, keepdims=True), squares.shape)
    r = lax.rsqrt((total + pltpu.roll(total, 4, 1)) * (1.0 / WIDTH) + EPS)
    low = lax.broadcasted_iota(jnp.int32, (1, 8, 128), 1) < 4
    for c in range(3):
        both = parts[c] * r * jnp.where(low, gain[c], gain[c + 3])
        left, right = swap4(*pairs(both))
        x_ref[512:576, 128 * c : 128 * c + 128] = left.reshape(64, 128).astype(BF16)
        x_ref[512:576, ATTN + 128 * c : ATTN + 128 * c + 128] = right.reshape(64, 128).astype(BF16)
    for b, cols in BLOCKS:
        w_copies[b].wait()
        proj_ref[:, cols] = jnp.dot(
            x_ref[...], w_ref[:, cols], preferred_element_type=F32
        ).astype(BF16)

    def mix(base, n):
        size = FRAMES * n
        row = lax.broadcasted_iota(jnp.int32, (1, size, size), 1)
        col = lax.broadcasted_iota(jnp.int32, (1, size, size), 2)
        kept = ((row & (n - 1)) == (col & (n - 1))) & (col // n <= row // n)
        lane = lax.broadcasted_iota(jnp.int32, (size, 128), 1) < 64
        one = jnp.where(lane, 1.0, 0.0).astype(BF16)
        other = jnp.where(lane, 0.0, 1.0).astype(BF16)
        results = []
        for h in range(3):
            q = proj_ref[base : base + size, 128 * h : 128 * h + 128]
            k = proj_ref[base : base + size, ATTN + 128 * h : ATTN + 128 * h + 128]
            v = proj_ref[base : base + size, 2 * ATTN + 128 * h : 2 * ATTN + 128 * h + 128]
            scores = lax.dot_general(
                jnp.concatenate([q * one, q * other], 0),
                k,
                (((1,), (1,)), ((), ())),
                preferred_element_type=F32,
            )
            scores = jnp.where(kept, scores.reshape(2, size, size) * 0.125, -1e30)
            expo = jnp.exp(scores - jnp.max(scores, axis=-1, keepdims=True))
            total = jnp.sum(expo, axis=-1, keepdims=True)
            weights = expo.reshape(2 * size, size).astype(BF16)
            mixed = jnp.dot(weights, v, preferred_element_type=F32).reshape(2, size, 128) / total
            results.append(jnp.where(lane, mixed[0], mixed[1]))
        return results

    for s in range(4):
        for h, mixed in enumerate(mix(128 * s, 8)):
            at = (s // 2) * 48 + 16 * h + 8 * (s % 2)
            mixed = mixed.reshape(FRAMES, 8, 128).astype(BF16)
            out_ref[0:15, at : at + 8, :] = mixed[1:16]
            out_ref[15:16, at : at + 8, :] = mixed[0:1]
    rest = [mixed.reshape(8, 8, 128) for mixed in mix(512, 4)]
    for at, (even, odd) in ((96, swap4(rest[0], rest[1])), (104, swap4(rest[2], rest[2]))):
        for i in range(8):
            out_ref[(2 * i - 1) % FRAMES, at : at + 8, :] = even[i].astype(BF16)
            out_ref[2 * i, at : at + 8, :] = odd[i].astype(BF16)


def put_chunks(values, out_ref):
    for c in range(6):
        block = values[:512, 128 * c : 128 * c + 128].reshape(LATS, 16, 128)
        out_ref[:, 16 * c : 16 * c + 16, :] = block.astype(BF16)
    slot = lax.broadcasted_iota(jnp.int32, (LATS, 8, 128), 1)
    for t in range(2):
        tile = None
        for q in range(3):
            at = 256 * q + 128 * t
            part = values[512:, at : at + 128].reshape(LATS, 8, 128)
            tile = part if tile is None else jnp.where(slot // 2 == q, part, tile)
        out_ref[:, 96 + 8 * t : 104 + 8 * t, :] = tile.astype(BF16)


def get_chunks(in_ref, rows_ref):
    for c in range(6):
        rows_ref[0:512, 128 * c : 128 * c + 128] = in_ref[:, 16 * c : 16 * c + 16, :].reshape(
            512, 128
        )
    slot = lax.broadcasted_iota(jnp.int32, (LATS, 8, 128), 1)
    for t in range(2):
        tile = in_ref[:, 96 + 8 * t : 104 + 8 * t, :].astype(F32)
        for q in range(3):
            at = 256 * q + 128 * t
            rows_ref[512:768, at : at + 128] = (
                jnp.where(slot // 2 == q, tile, 0.0).reshape(256, 128).astype(BF16)
            )


def to_spectra(
    frame_ref, params_ref, mixed_ref, window_any, w_any, tables_any,
    carry_any, out_ref, mixed_rows, base_rows, split_ref, window_ref, w_ref, table_ref, sems,
):
    w_copy = fetch(w_any, w_ref, sems.at[0])
    window_copy = fetch(window_any, window_ref, sems.at[1])
    table_copy = fetch(tables_any.at[0, :, 0:640], table_ref, sems.at[2])
    for block in range(2):
        for h in range(3):
            at = (block * 3 + h) * 16
            for d in range(FRAMES):
                mixed_rows[
                    32 * d + 16 * block : 32 * d + 16 * block + 16, 128 * h : 128 * h + 128
                ] = mixed_ref[d, at : at + 16, :]
    left, right = swap4(*pairs(mixed_ref[:, 96:104, :].astype(F32)))
    last, _ = swap4(*pairs(mixed_ref[:, 104:112, :].astype(F32)))
    for h, tile in enumerate((left, right, last)):
        mixed_rows[512:576, 128 * h : 128 * h + 128] = tile.reshape(64, 128).astype(BF16)
    scale = params_ref[frame_ref[0], 0:1, 0:1]
    gain = gain_row(params_ref, 1)
    w_copy.wait()
    window_copy.wait()
    first = window_ref[...].astype(F32) * scale + jnp.dot(
        mixed_rows[...], w_ref[...], preferred_element_type=F32
    )
    high = first.astype(BF16)
    split_ref[0] = high
    split_ref[1] = (first - high.astype(F32)).astype(BF16)
    carries = [
        fetch(split_ref, carry_any.at[0:2], sems.at[3]),
        fetch(window_ref, carry_any.at[2], sems.at[4]),
    ]
    base_rows[0:POINTS, :] = (first * row_scale(first) * gain).astype(BF16)
    base_rows[POINTS:640, :] = jnp.zeros((640 - POINTS, WIDTH), BF16)
    table_copy.wait()
    put_chunks(jnp.dot(table_ref[...], base_rows[...], preferred_element_type=F32), out_ref)
    for copy in carries:
        copy.wait()


def filter_orders(in_ref, down_ref, up_ref, filter_ref, out_ref, rows_ref, coeffs_ref):
    get_chunks(in_ref, rows_ref)
    factor = filter_ref[...].astype(F32)
    coeffs = jnp.dot(down_ref[...], rows_ref[...], preferred_element_type=F32)
    for b in range(2 * ORDERS):
        rows = slice(LMAX * b, LMAX * (b + 1))
        coeffs_ref[rows, :] = (coeffs[rows] * factor).astype(BF16)
    put_chunks(jnp.dot(up_ref[...], coeffs_ref[...], preferred_element_type=F32), out_ref)


def gelu(x):
    return 0.5 * x * (1.0 + jnp.tanh(np.float32(np.sqrt(2 / np.pi)) * (x + 0.044715 * (x * x * x))))


def feed_forward(
    frame_ref, params_ref, in_any, tables_any, carry_any, *refs
):
    shards, refs = refs[:SHARDS], refs[SHARDS:]
    (
        out_any, rows_ref, inner_ref, hidden_ref, out_ref, table_ref, carry_ref, second_ref,
        w_ref, in_ref, sems, w_sems,
    ) = refs
    in_copy = fetch(in_any, in_ref, sems.at[2])
    table_copy = fetch(tables_any.at[1, 0:POINTS], table_ref, sems.at[0])
    first_copy = fetch(carry_any.at[0:2], carry_ref.at[0:2], sems.at[1])
    in_copy.wait()
    get_chunks(in_ref, rows_ref)
    w_copies, at = [], 0
    for i, shard in enumerate(shards):
        w_copies.append(fetch(shard, w_ref.at[at : at + shard.shape[0]], w_sems.at[i]))
        at += shard.shape[0]
    gain = gain_row(params_ref, 2)
    table_copy.wait()
    second_ref[...] = jnp.dot(table_ref[...], rows_ref[...], preferred_element_type=F32)
    first_copy.wait()
    window_copy = fetch(carry_any.at[2], carry_ref.at[2], sems.at[4])
    second = carry_ref[0].astype(F32) + carry_ref[1].astype(F32) + second_ref[...]
    second_ref[...] = second
    inner_ref[...] = (second * row_scale(second) * gain).astype(BF16)
    for b in range(2):
        units = slice(8 * b, 8 * b + 8)
        for copy in w_copies[4 * b : 4 * b + 4] if b == 0 else w_copies[4:]:
            copy.wait()
        raised = lax.dot_general(
            inner_ref[...],
            w_ref[units, 0:96, :].reshape(FF // 2, WIDTH),
            (((1,), (1,)), ((), ())),
            preferred_element_type=F32,
        )
        hidden_ref[:, FF // 2 * b : FF // 2 * (b + 1)] = gelu(raised).astype(BF16)
    ratio = params_ref[FRAMES + frame_ref[0], 0:1, 0:1]
    window_copy.wait()
    w_down = w_ref[:, 96:192, :].reshape(FF, WIDTH)
    copies = []
    for j in range(2):
        rows = slice(POINTS // 2 * j, POINTS // 2 * (j + 1))
        denoised = second_ref[rows, :] + jnp.dot(
            hidden_ref[rows, :], w_down, preferred_element_type=F32
        )
        state = carry_ref[2, rows, :].astype(F32)
        out_ref[rows, :] = (denoised + ratio * (state - denoised)).astype(BF16)
        copies.append(fetch(out_ref.at[rows], out_any.at[rows], sems.at[5 + j]))
    for copy in copies:
        copy.wait()


SPACES = {"v": pltpu.VMEM, "s": pltpu.SMEM, "h": pltpu.HBM}


def call(kernel, outs, kinds, scratch, args, flops, limit):
    specs = [pl.BlockSpec(memory_space=SPACES[kind]) for kind in kinds]
    return pl.pallas_call(
        kernel,
        out_shape=outs,
        in_specs=specs[: len(args)],
        out_specs=specs[len(args) :],
        scratch_shapes=[
            pltpu.VMEM(*entry) if isinstance(entry, tuple) else pltpu.SemaphoreType.DMA((entry,))
            for entry in scratch
        ],
        compiler_params=pltpu.CompilerParams(vmem_limit_bytes=int(limit * MIB)),
        cost_estimate=pl.CostEstimate(
            flops=flops,
            bytes_accessed=sum(a.size * a.dtype.itemsize for a in list(args) + outs),
            transcendentals=0,
        ),
    )(*args)


def exchange(chunks, axis):
    return lax.all_to_all(chunks, axis, split_axis=0, concat_axis=0, tiled=True)


def shift(value, steps):
    hops = [(source, (source + steps) % FRAMES) for source in range(FRAMES)]
    return lax.ppermute(value, "lead", hops)


def swap_cores(value):
    return lax.ppermute(value, "lead", [(source, source ^ 1) for source in range(FRAMES)])


def round_chips(value, chips):
    hops = [(s, (s + (2 * chips if s % 2 == 0 else -2 * chips)) % FRAMES) for s in range(FRAMES)]
    return lax.ppermute(value, "lead", hops)


def per_device(
    window, noise_level, keep_ratio, norm_gains, w_qkv, w_out, spectral_filter, w_in, w_down
):
    lead, lat = lax.axis_index("lead"), lax.axis_index("lat")
    frame = ((lead + 1) & (FRAMES - 1)).astype(jnp.int32).reshape(1)
    tables = jnp.asarray(fourier_tables())
    legendre = jnp.asarray(legendre_tables())
    placement = jnp.asarray(placement_table())
    shape = jax.ShapeDtypeStruct

    state = window.reshape(POINTS, WIDTH)
    packed, params = call(
        pack_window,
        [shape((FRAMES, 9, 8, ATTN), BF16), shape((2 * FRAMES + 3, 8, 128), F32)],
        "ssvvvv",
        [],
        [noise_level, keep_ratio, norm_gains, window.reshape(18, 4, 8, WIDTH)],
        0,
        LIMITS[0],
    )
    ahead = shift(state, -1)
    packed, legendre, w_in, w_down = lax.optimization_barrier((packed, legendre, w_in, w_down))
    own = jnp.concatenate([w_in, w_down], 0)[None]
    other = swap_cores(own)
    pair = jnp.where(
        lead % 2 == 0, jnp.concatenate([own, other], 0), jnp.concatenate([other, own], 0)
    )
    local = lax.dynamic_slice_in_dim(legendre, ORDERS * lat, ORDERS, 1)
    down = jnp.einsum("ilj,icjn->icln", local[0], placement, preferred_element_type=F32)
    down = down.astype(BF16).reshape(2 * ORDERS * LMAX, 768)
    up = jnp.einsum("ilj,icjn->nicl", local[1], placement, preferred_element_type=F32)
    up = up.astype(BF16).reshape(768, 2 * ORDERS * LMAX)

    (mixed,) = call(
        attend,
        [shape((FRAMES, 112, 128), BF16)],
        "vvhv",
        [((POINTS, WIDTH), BF16), ((POINTS, 3 * ATTN), BF16), ((WIDTH, 3 * ATTN), BF16), 3],
        [params, exchange(packed, "lead"), w_qkv],
        2 * POINTS * WIDTH * 3 * ATTN,
        LIMITS[1],
    )
    mixed, ahead, pair = lax.optimization_barrier((mixed, ahead, pair))
    mixed = exchange(mixed, "lead")
    carry, spectra = call(
        to_spectra,
        [shape((3, POINTS, WIDTH), BF16), shape((LATS, 112, 128), BF16)],
        "svvhhhhv",
        [
            ((POINTS, ATTN), BF16),
            ((640, WIDTH), BF16),
            ((2, POINTS, WIDTH), BF16),
            ((POINTS, WIDTH), BF16),
            ((ATTN, WIDTH), BF16),
            ((768, 640), BF16),
            5,
        ],
        [frame, params, mixed, ahead, w_out, tables],
        2 * POINTS * WIDTH * (ATTN + 768),
        LIMITS[2],
    )
    spectra, pair = lax.optimization_barrier((spectra, pair))
    first_pair, second_pair = round_chips(pair, 1), round_chips(pair, 2)
    swapped = swap_cores(first_pair)
    by_order = exchange(spectra, "lat")
    by_order, second_pair, swapped = lax.optimization_barrier((by_order, second_pair, swapped))
    shards = [pair, first_pair, swapped, second_pair]
    (back,) = call(
        filter_orders,
        [shape((LATS, 112, 128), BF16)],
        "vvvvv",
        [((768, WIDTH), BF16), ((2 * ORDERS * LMAX, WIDTH), BF16)],
        [by_order, down, up, spectral_filter],
        4 * POINTS * WIDTH * 768,
        LIMITS[3],
    )
    back, second_pair = lax.optimization_barrier((back, second_pair))
    third_pair = round_chips(second_pair, 1)
    last = round_chips(jnp.where(lead % 2 == 0, second_pair[0:1], second_pair[1:2]), 2)
    shards += [third_pair, swap_cores(second_pair), swap_cores(third_pair), last, swap_cores(last)]
    (stepped,) = call(
        feed_forward,
        [shape((POINTS, WIDTH), BF16)],
        "svhhh" + "h" * SHARDS + "h",
        [
            ((768, WIDTH), BF16),
            ((POINTS, WIDTH), BF16),
            ((POINTS, FF), BF16),
            ((POINTS, WIDTH), BF16),
            ((POINTS, 768), BF16),
            ((3, POINTS, WIDTH), BF16),
            ((POINTS, WIDTH), F32),
            ((FRAMES, 192, WIDTH), BF16),
            ((LATS, 112, 128), BF16),
            7,
            SHARDS,
        ],
        [frame, params, exchange(back, "lat"), tables, carry, *shards],
        2 * POINTS * WIDTH * (2 * FF + 768),
        LIMITS[4],
    )
    return stepped.reshape(1, ROWS, NLON, WIDTH)


def solution(mesh):
    return jax.shard_map(
        per_device,
        mesh=mesh,
        in_specs=(
            P("lead", "lat", None, None),
            P(),
            P(),
            P(),
            P(),
            P(),
            P(),
            P("lead", None),
            P("lead", None),
        ),
        out_specs=P("lead", "lat", None, None),
        check_vma=False,
    )
```

```python
import jax
import jax.numpy as jnp
import ml_dtypes
import numpy as np
from jax import lax
from jax.experimental import pallas as pl
from jax.experimental.pallas import tpu as pltpu
from jax.sharding import PartitionSpec as P

F32, BF16 = jnp.float32, jnp.bfloat16
FRAMES, LATS, ROWS, NLON, NLAT, LMAX = 16, 32, 3, 192, 96, 96
POINTS, WIDTH, ATTN, FF = ROWS * NLON, 768, 384, 1536
ORDERS = LMAX // LATS
EPS = 1e-05
SHARDS = 9
BLOCKS = tuple((b, slice(ATTN * b, ATTN * (b + 1))) for b in range(3))
MIB = 1 << 20
LIMITS = (60, 51, 52, 16, 49)


def chunk_row(r):
    return r // 6, (r // 2) % 3, r % 2


def chunk_columns():
    listed = [(d,) + chunk_row(r) for d in range(LATS) for r in range(16)]
    for d in range(LATS):
        listed += [(d,) + chunk_row(16 + s % 2) if s < 6 else None for s in range(8)]
    return listed


def fourier_tables():
    forward = np.zeros((768, ROWS, NLON))
    inverse = np.zeros((768, ROWS, NLON))
    lon = np.arange(NLON)
    for at, entry in enumerate(chunk_columns()):
        if entry is None:
            continue
        owner, j, i, c = entry
        m = ORDERS * owner + i
        angle = 2 * np.pi * ((m * lon) % NLON) / NLON
        wave = np.cos(angle) if c == 0 else -np.sin(angle)
        forward[at, j] = wave
        inverse[at, j] = wave * (1.0 if m == 0 else 2.0)
    tables = np.zeros((2, 768, 768))
    tables[0, :, :POINTS] = forward.reshape(768, POINTS)
    tables[1, :POINTS] = inverse.reshape(768, POINTS).T
    return tables.astype(ml_dtypes.bfloat16)


def placement_table():
    table = np.zeros((ORDERS, 2, NLAT, 768))
    for at, entry in enumerate(chunk_columns()):
        if entry is not None:
            source, j, i, c = entry
            table[i, c, ROWS * source + j, at] = 1.0
    return table.astype(ml_dtypes.bfloat16)


def legendre_tables():
    colatitude = np.pi * (np.arange(NLAT) + 0.5) / NLAT
    cosines = np.cos(colatitude)
    sine_rows = np.sin(colatitude)
    legendre = np.zeros((LMAX, LMAX, NLAT))
    for order_m in range(LMAX):
        counter = np.arange(1, order_m + 1)
        log_part = (
            0.5 * np.log((2 * order_m + 1) / (4 * np.pi))
            + 0.5 * np.sum(np.log((2 * counter - 1) / (2 * counter)))
            + order_m * np.log(sine_rows)
        )
        diagonal_value = (-1.0) ** order_m * np.exp(log_part)
        legendre[order_m, order_m] = diagonal_value
        if order_m + 1 < LMAX:
            legendre[order_m, order_m + 1] = cosines * np.sqrt(2 * order_m + 3) * diagonal_value
        for degree_l in range(order_m + 2, LMAX):
            factor_a = np.sqrt(
                (4.0 * degree_l * degree_l - 1) / (degree_l * degree_l - order_m * order_m)
            )
            factor_b = np.sqrt(
                ((degree_l - 1.0) ** 2 - order_m * order_m) / (4.0 * (degree_l - 1) ** 2 - 1)
            )
            legendre[order_m, degree_l] = factor_a * (
                cosines * legendre[order_m, degree_l - 1]
                - factor_b * legendre[order_m, degree_l - 2]
            )
    quadrature = sine_rows * (np.pi / NLAT) * (2 * np.pi / NLON)
    return np.stack([legendre * quadrature, legendre]).astype(ml_dtypes.bfloat16)


def swap4(first, second):
    low = lax.broadcasted_iota(jnp.int32, first.shape, 1) < 4
    rolled_first, rolled_second = pltpu.roll(first, 4, 1), pltpu.roll(second, 4, 1)
    return jnp.where(low, first, rolled_second), jnp.where(low, rolled_first, second)


def pairs(tiles):
    split = tiles.reshape(8, 2, 8, 128)
    return split[:, 0], split[:, 1]


def fetch(source, target, sem):
    copy = pltpu.make_async_copy(source, target, sem)
    copy.start()
    return copy


def row_scale(values):
    return lax.rsqrt(jnp.sum(values * values, axis=-1, keepdims=True) * (1.0 / WIDTH) + EPS)


def bundle(noise_ref, keep_ref, gains_ref, params_ref):
    for f in range(FRAMES):
        level = jnp.full((8, 128), noise_ref[f], F32)
        params_ref[f] = lax.rsqrt(1.0 + level * level)
        params_ref[FRAMES + f] = jnp.full((8, 128), 0.0 if f == 0 else keep_ref[f], F32)
    for norm in range(3):
        for c in range(6):
            params_ref[2 * FRAMES + norm, c : c + 1, :] = gains_ref[
                norm : norm + 1, 128 * c : 128 * c + 128
            ]


def pack_window(window_ref, out_ref):
    for h in range(2):
        out_ref[:, 4 * h : 4 * h + 4] = window_ref[0:16, :, :, ATTN * h : ATTN * h + ATTN]
    for c in range(3):
        left = window_ref[16:18, :, :, 128 * c : 128 * c + 128].astype(F32).reshape(8, 8, 128)
        right = window_ref[16:18, :, :, ATTN + 128 * c : ATTN + 128 * c + 128].astype(F32)
        even, odd = swap4(left, right.reshape(8, 8, 128))
        for i in range(8):
            out_ref[2 * i, 8, :, 128 * c : 128 * c + 128] = even[i].astype(BF16)
            out_ref[2 * i + 1, 8, :, 128 * c : 128 * c + 128] = odd[i].astype(BF16)


def gain_row(params_ref, norm):
    return jnp.concatenate([params_ref[2 * FRAMES + norm, c : c + 1, :] for c in range(6)], 1)


def attend(params_ref, in_ref, w_any, out_ref, x_ref, proj_ref, w_ref, sems):
    w_copies = [fetch(w_any.at[:, cols], w_ref.at[:, cols], sems.at[b]) for b, cols in BLOCKS]
    scale = params_ref[0:FRAMES]
    gain = [params_ref[2 * FRAMES, c : c + 1, :].reshape(1, 1, 128) for c in range(6)]
    for s in range(4):
        parts = [
            in_ref[:, 4 * (c // 3) + s, :, 128 * (c % 3) : 128 * (c % 3) + 128].astype(F32) * scale
            for c in range(6)
        ]
        squares = sum(v * v for v in parts)
        r = lax.rsqrt(jnp.sum(squares, axis=-1, keepdims=True) * (1.0 / WIDTH) + EPS)
        for c in range(6):
            x_ref[128 * s : 128 * s + 128, 128 * c : 128 * c + 128] = (
                (parts[c] * r * gain[c]).reshape(128, 128).astype(BF16)
            )
    parts = [in_ref[:, 8, :, 128 * c : 128 * c + 128].astype(F32) * scale for c in range(3)]
    squares = sum(v * v for v in parts)
    total = jnp.broadcast_to(jnp.sum(squares, axis=-1, keepdims=True), squares.shape)
    r = lax.rsqrt((total + pltpu.roll(total, 4, 1)) * (1.0 / WIDTH) + EPS)
    low = lax.broadcasted_iota(jnp.int32, (1, 8, 128), 1) < 4
    for c in range(3):
        both = parts[c] * r * jnp.where(low, gain[c], gain[c + 3])
        left, right = swap4(*pairs(both))
        x_ref[512:576, 128 * c : 128 * c + 128] = left.reshape(64, 128).astype(BF16)
        x_ref[512:576, ATTN + 128 * c : ATTN + 128 * c + 128] = right.reshape(64, 128).astype(BF16)
    for b, cols in BLOCKS:
        w_copies[b].wait()
        proj_ref[:, cols] = jnp.dot(
            x_ref[...], w_ref[:, cols], preferred_element_type=F32
        ).astype(BF16)

    def mix(base, n):
        size = FRAMES * n
        row = lax.broadcasted_iota(jnp.int32, (1, size, size), 1)
        col = lax.broadcasted_iota(jnp.int32, (1, size, size), 2)
        kept = ((row & (n - 1)) == (col & (n - 1))) & (col // n <= row // n)
        lane = lax.broadcasted_iota(jnp.int32, (size, 128), 1) < 64
        one = jnp.where(lane, 1.0, 0.0).astype(BF16)
        other = jnp.where(lane, 0.0, 1.0).astype(BF16)
        results = []
        for h in range(3):
            q = proj_ref[base : base + size, 128 * h : 128 * h + 128]
            k = proj_ref[base : base + size, ATTN + 128 * h : ATTN + 128 * h + 128]
            v = proj_ref[base : base + size, 2 * ATTN + 128 * h : 2 * ATTN + 128 * h + 128]
            scores = lax.dot_general(
                jnp.concatenate([q * one, q * other], 0),
                k,
                (((1,), (1,)), ((), ())),
                preferred_element_type=F32,
            )
            scores = jnp.where(kept, scores.reshape(2, size, size) * 0.125, -1e30)
            expo = jnp.exp(scores - jnp.max(scores, axis=-1, keepdims=True))
            total = jnp.sum(expo, axis=-1, keepdims=True)
            weights = expo.reshape(2 * size, size).astype(BF16)
            mixed = jnp.dot(weights, v, preferred_element_type=F32).reshape(2, size, 128) / total
            results.append(jnp.where(lane, mixed[0], mixed[1]))
        return results

    for s in range(4):
        for h, mixed in enumerate(mix(128 * s, 8)):
            at = (s // 2) * 48 + 16 * h + 8 * (s % 2)
            mixed = mixed.reshape(FRAMES, 8, 128).astype(BF16)
            out_ref[0:15, at : at + 8, :] = mixed[1:16]
            out_ref[15:16, at : at + 8, :] = mixed[0:1]
    rest = [mixed.reshape(8, 8, 128) for mixed in mix(512, 4)]
    for at, (even, odd) in ((96, swap4(rest[0], rest[1])), (104, swap4(rest[2], rest[2]))):
        for i in range(8):
            out_ref[(2 * i - 1) % FRAMES, at : at + 8, :] = even[i].astype(BF16)
            out_ref[2 * i, at : at + 8, :] = odd[i].astype(BF16)


def put_chunks(columns, out_ref, out_any, sems):
    slot = lax.broadcasted_iota(jnp.int32, (LATS, 8, 128), 1)
    tiles, copies = [None, None], []
    for q in range(3):
        values = columns(q)
        for t in range(2):
            at = 32 * q + 16 * t
            block = values[:512, 128 * t : 128 * t + 128].reshape(LATS, 16, 128)
            out_ref[:, at : at + 16, :] = block.astype(BF16)
            part = values[512:, 128 * t : 128 * t + 128].reshape(LATS, 8, 128)
            tiles[t] = part if q == 0 else jnp.where(slot // 2 == q, part, tiles[t])
        if q == 2:
            for t in range(2):
                out_ref[:, 96 + 8 * t : 104 + 8 * t, :] = tiles[t].astype(BF16)
        rows = slice(32 * q, 32 * q + (32 if q < 2 else 48))
        copies.append(fetch(out_ref.at[:, rows, :], out_any.at[:, rows, :], sems.at[q]))
    return copies


def get_chunks(in_ref, rows_ref):
    for c in range(6):
        rows_ref[0:512, 128 * c : 128 * c + 128] = in_ref[:, 16 * c : 16 * c + 16, :].reshape(
            512, 128
        )
    slot = lax.broadcasted_iota(jnp.int32, (LATS, 8, 128), 1)
    for t in range(2):
        tile = in_ref[:, 96 + 8 * t : 104 + 8 * t, :].astype(F32)
        for q in range(3):
            at = 256 * q + 128 * t
            rows_ref[512:768, at : at + 128] = (
                jnp.where(slot // 2 == q, tile, 0.0).reshape(256, 128).astype(BF16)
            )


def to_spectra(
    frame_ref, params_ref, mixed_ref, window_any, w_any, tables_any,
    carry_any, out_any, out_ref, mixed_rows, base_rows, kept_ref, window_ref, w_ref, table_ref, sems, out_sems,
):
    w_copy = fetch(w_any, w_ref, sems.at[0])
    window_copy = fetch(window_any, window_ref, sems.at[1])
    table_copy = fetch(tables_any.at[0, :, 0:640], table_ref, sems.at[2])
    for block in range(2):
        for h in range(3):
            at = (block * 3 + h) * 16
            for d in range(FRAMES):
                mixed_rows[
                    32 * d + 16 * block : 32 * d + 16 * block + 16, 128 * h : 128 * h + 128
                ] = mixed_ref[d, at : at + 16, :]
    left, right = swap4(*pairs(mixed_ref[:, 96:104, :].astype(F32)))
    last, _ = swap4(*pairs(mixed_ref[:, 104:112, :].astype(F32)))
    for h, tile in enumerate((left, right, last)):
        mixed_rows[512:576, 128 * h : 128 * h + 128] = tile.reshape(64, 128).astype(BF16)
    scale = params_ref[frame_ref[0], 0:1, 0:1]
    gain = gain_row(params_ref, 1)
    w_copy.wait()
    window_copy.wait()
    first = window_ref[...].astype(F32) * scale + jnp.dot(
        mixed_rows[...], w_ref[...], preferred_element_type=F32
    )
    kept_ref[...] = first.astype(BF16)
    carries = [
        fetch(kept_ref, carry_any.at[0], sems.at[3]),
        fetch(window_ref, carry_any.at[1], sems.at[4]),
    ]
    base_rows[0:POINTS, :] = (first * row_scale(first) * gain).astype(BF16)
    base_rows[POINTS:640, :] = jnp.zeros((640 - POINTS, WIDTH), BF16)
    table_copy.wait()

    def columns(q):
        cols = slice(256 * q, 256 * q + 256)
        return jnp.dot(table_ref[...], base_rows[:, cols], preferred_element_type=F32)

    for copy in carries + put_chunks(columns, out_ref, out_any, out_sems):
        copy.wait()


def filter_orders(in_ref, down_ref, up_ref, out_any, out_ref, rows_ref, coeffs_ref, sems):
    get_chunks(in_ref, rows_ref)
    degrees = 2 * ORDERS * LMAX
    factor = down_ref[degrees : degrees + LMAX, :].astype(F32)
    coeffs = jnp.dot(down_ref[0:degrees, :], rows_ref[...], preferred_element_type=F32)
    for b in range(2 * ORDERS):
        rows = slice(LMAX * b, LMAX * (b + 1))
        coeffs_ref[rows, :] = (coeffs[rows] * factor).astype(BF16)
    values = jnp.dot(up_ref[...], coeffs_ref[...], preferred_element_type=F32)
    for copy in put_chunks(lambda q: values[:, 256 * q : 256 * q + 256], out_ref, out_any, sems):
        copy.wait()


def gelu(x):
    return 0.5 * x * (1.0 + jnp.tanh(np.float32(np.sqrt(2 / np.pi)) * (x + 0.044715 * (x * x * x))))


def feed_forward(
    frame_ref, params_ref, in_any, tables_any, carry_any, *refs
):
    shards, refs = refs[:SHARDS], refs[SHARDS:]
    (
        out_any, rows_ref, inner_ref, hidden_ref, out_ref, table_ref, carry_ref, second_ref,
        w_ref, in_ref, sems, w_sems,
    ) = refs
    in_copy = fetch(in_any, in_ref, sems.at[2])
    table_copy = fetch(tables_any.at[1, 0:POINTS], table_ref, sems.at[0])
    first_copy = fetch(carry_any.at[0], carry_ref.at[0], sems.at[1])
    in_copy.wait()
    get_chunks(in_ref, rows_ref)
    w_copies, at = [], 0
    for i, shard in enumerate(shards):
        w_copies.append(fetch(shard, w_ref.at[at : at + shard.shape[0]], w_sems.at[i]))
        at += shard.shape[0]
    gain = gain_row(params_ref, 2)
    table_copy.wait()
    second_ref[...] = jnp.dot(table_ref[...], rows_ref[...], preferred_element_type=F32)
    first_copy.wait()
    window_copy = fetch(carry_any.at[1], carry_ref.at[1], sems.at[4])
    second = carry_ref[0].astype(F32) + second_ref[...]
    second_ref[...] = second
    inner_ref[...] = (second * row_scale(second) * gain).astype(BF16)
    for b in range(2):
        units = slice(8 * b, 8 * b + 8)
        for copy in w_copies[4 * b : 4 * b + 4] if b == 0 else w_copies[4:]:
            copy.wait()
        raised = lax.dot_general(
            inner_ref[...],
            w_ref[units, 0:96, :].reshape(FF // 2, WIDTH),
            (((1,), (1,)), ((), ())),
            preferred_element_type=F32,
        )
        hidden_ref[:, FF // 2 * b : FF // 2 * (b + 1)] = gelu(raised).astype(BF16)
    ratio = params_ref[FRAMES + frame_ref[0], 0:1, 0:1]
    window_copy.wait()
    w_down = w_ref[:, 96:192, :].reshape(FF, WIDTH)
    copies = []
    for j in range(2):
        rows = slice(POINTS // 2 * j, POINTS // 2 * (j + 1))
        denoised = second_ref[rows, :] + jnp.dot(
            hidden_ref[rows, :], w_down, preferred_element_type=F32
        )
        state = carry_ref[1, rows, :].astype(F32)
        out_ref[rows, :] = (denoised + ratio * (state - denoised)).astype(BF16)
        copies.append(fetch(out_ref.at[rows], out_any.at[rows], sems.at[5 + j]))
    for copy in copies:
        copy.wait()


SPACES = {"v": pltpu.VMEM, "s": pltpu.SMEM, "h": pltpu.HBM}


def call(kernel, outs, kinds, scratch, args, flops, limit):
    specs = [pl.BlockSpec(memory_space=SPACES[kind]) for kind in kinds]
    return pl.pallas_call(
        kernel,
        out_shape=outs,
        in_specs=specs[: len(args)],
        out_specs=specs[len(args) :],
        scratch_shapes=[
            pltpu.VMEM(*entry) if isinstance(entry, tuple) else pltpu.SemaphoreType.DMA((entry,))
            for entry in scratch
        ],
        compiler_params=pltpu.CompilerParams(vmem_limit_bytes=int(limit * MIB)),
        cost_estimate=pl.CostEstimate(
            flops=flops,
            bytes_accessed=sum(a.size * a.dtype.itemsize for a in list(args) + outs),
            transcendentals=0,
        ),
    )(*args)


def exchange(chunks, axis):
    return lax.all_to_all(chunks, axis, split_axis=0, concat_axis=0, tiled=True)


def shift(value, steps):
    hops = [(source, (source + steps) % FRAMES) for source in range(FRAMES)]
    return lax.ppermute(value, "lead", hops)


def swap_cores(value):
    return lax.ppermute(value, "lead", [(source, source ^ 1) for source in range(FRAMES)])


def round_chips(value, chips):
    hops = [(s, (s + (2 * chips if s % 2 == 0 else -2 * chips)) % FRAMES) for s in range(FRAMES)]
    return lax.ppermute(value, "lead", hops)


def per_device(
    window, noise_level, keep_ratio, norm_gains, w_qkv, w_out, spectral_filter, w_in, w_down
):
    lead, lat = lax.axis_index("lead"), lax.axis_index("lat")
    frame = ((lead + 1) & (FRAMES - 1)).astype(jnp.int32).reshape(1)
    tables = jnp.asarray(fourier_tables())
    legendre = jnp.asarray(legendre_tables())
    placement = jnp.asarray(placement_table())
    shape = jax.ShapeDtypeStruct

    state = window.reshape(POINTS, WIDTH)
    (packed,) = call(
        pack_window,
        [shape((FRAMES, 9, 8, ATTN), BF16)],
        "vv",
        [],
        [window.reshape(18, 4, 8, WIDTH)],
        0,
        LIMITS[0],
    )
    ahead = shift(state, -1)
    packed, legendre, w_in, w_down, norm_gains = lax.optimization_barrier(
        (packed, legendre, w_in, w_down, norm_gains)
    )
    (params,) = call(
        bundle,
        [shape((2 * FRAMES + 3, 8, 128), F32)],
        "ssvv",
        [],
        [noise_level, keep_ratio, norm_gains],
        0,
        4,
    )
    own = jnp.concatenate([w_in, w_down], 0)[None]
    other = swap_cores(own)
    pair = jnp.where(
        lead % 2 == 0, jnp.concatenate([own, other], 0), jnp.concatenate([other, own], 0)
    )
    local = lax.dynamic_slice_in_dim(legendre, ORDERS * lat, ORDERS, 1)
    down = jnp.einsum("ilj,icjn->icln", local[0], placement, preferred_element_type=F32)
    down = down.astype(BF16).reshape(2 * ORDERS * LMAX, 768)
    down = jnp.concatenate([down, spectral_filter], 0)
    up = jnp.einsum("ilj,icjn->nicl", local[1], placement, preferred_element_type=F32)
    up = up.astype(BF16).reshape(768, 2 * ORDERS * LMAX)

    (mixed,) = call(
        attend,
        [shape((FRAMES, 112, 128), BF16)],
        "vvhv",
        [((POINTS, WIDTH), BF16), ((POINTS, 3 * ATTN), BF16), ((WIDTH, 3 * ATTN), BF16), 3],
        [params, exchange(packed, "lead"), w_qkv],
        2 * POINTS * WIDTH * 3 * ATTN,
        LIMITS[1],
    )
    mixed, ahead, pair = lax.optimization_barrier((mixed, ahead, pair))
    mixed = exchange(mixed, "lead")
    carry, spectra = call(
        to_spectra,
        [shape((2, POINTS, WIDTH), BF16), shape((LATS, 112, 128), BF16)],
        "svvhhhhh",
        [
            ((LATS, 112, 128), BF16),
            ((POINTS, ATTN), BF16),
            ((640, WIDTH), BF16),
            ((POINTS, WIDTH), BF16),
            ((POINTS, WIDTH), BF16),
            ((ATTN, WIDTH), BF16),
            ((768, 640), BF16),
            5,
            3,
        ],
        [frame, params, mixed, ahead, w_out, tables],
        2 * POINTS * WIDTH * (ATTN + 768),
        LIMITS[2],
    )
    spectra, pair = lax.optimization_barrier((spectra, pair))
    first_pair, second_pair = round_chips(pair, 1), round_chips(pair, 2)
    swapped = swap_cores(first_pair)
    by_order = exchange(spectra, "lat")
    by_order, second_pair, swapped = lax.optimization_barrier((by_order, second_pair, swapped))
    shards = [pair, first_pair, swapped, second_pair]
    (back,) = call(
        filter_orders,
        [shape((LATS, 112, 128), BF16)],
        "vvvh",
        [
            ((LATS, 112, 128), BF16),
            ((768, WIDTH), BF16),
            ((2 * ORDERS * LMAX, WIDTH), BF16),
            3,
        ],
        [by_order, down, up],
        4 * POINTS * WIDTH * 768,
        LIMITS[3],
    )
    back, second_pair = lax.optimization_barrier((back, second_pair))
    third_pair = round_chips(second_pair, 1)
    last = round_chips(jnp.where(lead % 2 == 0, second_pair[0:1], second_pair[1:2]), 2)
    shards += [third_pair, swap_cores(second_pair), swap_cores(third_pair), last, swap_cores(last)]
    (stepped,) = call(
        feed_forward,
        [shape((POINTS, WIDTH), BF16)],
        "svhhh" + "h" * SHARDS + "h",
        [
            ((768, WIDTH), BF16),
            ((POINTS, WIDTH), BF16),
            ((POINTS, FF), BF16),
            ((POINTS, WIDTH), BF16),
            ((POINTS, 768), BF16),
            ((2, POINTS, WIDTH), BF16),
            ((POINTS, WIDTH), F32),
            ((FRAMES, 192, WIDTH), BF16),
            ((LATS, 112, 128), BF16),
            7,
            SHARDS,
        ],
        [frame, params, exchange(back, "lat"), tables, carry, *shards],
        2 * POINTS * WIDTH * (2 * FF + 768),
        LIMITS[4],
    )
    return stepped.reshape(1, ROWS, NLON, WIDTH)


def solution(mesh):
    return jax.shard_map(
        per_device,
        mesh=mesh,
        in_specs=(
            P("lead", "lat", None, None),
            P(),
            P(),
            P(),
            P(),
            P(),
            P(),
            P("lead", None),
            P("lead", None),
        ),
        out_specs=P("lead", "lat", None, None),
        check_vma=False,
    )
```

```python
import jax
import jax.numpy as jnp
import ml_dtypes
import numpy as np
from jax import lax
from jax.experimental import pallas as pl
from jax.experimental.pallas import tpu as pltpu
from jax.sharding import PartitionSpec as P

F32, BF16 = jnp.float32, jnp.bfloat16
FRAMES, LATS, ROWS, NLON, NLAT, LMAX = 16, 32, 3, 192, 96, 96
POINTS, WIDTH, ATTN, FF = ROWS * NLON, 768, 384, 1536
ORDERS = LMAX // LATS
EPS = 1e-05
SHARDS = 9
BLOCKS = tuple((b, slice(ATTN * b, ATTN * (b + 1))) for b in range(3))
MIB = 1 << 20
LIMITS = (60, 51, 52, 16, 49)


def chunk_row(r):
    return r // 6, (r // 2) % 3, r % 2


def chunk_columns():
    listed = [(d,) + chunk_row(r) for d in range(LATS) for r in range(16)]
    for d in range(LATS):
        listed += [(d,) + chunk_row(16 + s % 2) if s < 6 else None for s in range(8)]
    return listed


def fourier_tables():
    forward = np.zeros((768, ROWS, NLON))
    inverse = np.zeros((768, ROWS, NLON))
    lon = np.arange(NLON)
    for at, entry in enumerate(chunk_columns()):
        if entry is None:
            continue
        owner, j, i, c = entry
        m = ORDERS * owner + i
        angle = 2 * np.pi * ((m * lon) % NLON) / NLON
        wave = np.cos(angle) if c == 0 else -np.sin(angle)
        forward[at, j] = wave
        inverse[at, j] = wave * (1.0 if m == 0 else 2.0)
    tables = np.zeros((2, 768, 768))
    tables[0, :, :POINTS] = forward.reshape(768, POINTS)
    tables[1, :POINTS] = inverse.reshape(768, POINTS).T
    return tables.astype(ml_dtypes.bfloat16)


def placement_table():
    table = np.zeros((ORDERS, 2, NLAT, 768))
    for at, entry in enumerate(chunk_columns()):
        if entry is not None:
            source, j, i, c = entry
            table[i, c, ROWS * source + j, at] = 1.0
    return table.astype(ml_dtypes.bfloat16)


def legendre_tables():
    colatitude = np.pi * (np.arange(NLAT) + 0.5) / NLAT
    cosines = np.cos(colatitude)
    sine_rows = np.sin(colatitude)
    legendre = np.zeros((LMAX, LMAX, NLAT))
    for order_m in range(LMAX):
        counter = np.arange(1, order_m + 1)
        log_part = (
            0.5 * np.log((2 * order_m + 1) / (4 * np.pi))
            + 0.5 * np.sum(np.log((2 * counter - 1) / (2 * counter)))
            + order_m * np.log(sine_rows)
        )
        diagonal_value = (-1.0) ** order_m * np.exp(log_part)
        legendre[order_m, order_m] = diagonal_value
        if order_m + 1 < LMAX:
            legendre[order_m, order_m + 1] = cosines * np.sqrt(2 * order_m + 3) * diagonal_value
        for degree_l in range(order_m + 2, LMAX):
            factor_a = np.sqrt(
                (4.0 * degree_l * degree_l - 1) / (degree_l * degree_l - order_m * order_m)
            )
            factor_b = np.sqrt(
                ((degree_l - 1.0) ** 2 - order_m * order_m) / (4.0 * (degree_l - 1) ** 2 - 1)
            )
            legendre[order_m, degree_l] = factor_a * (
                cosines * legendre[order_m, degree_l - 1]
                - factor_b * legendre[order_m, degree_l - 2]
            )
    quadrature = sine_rows * (np.pi / NLAT) * (2 * np.pi / NLON)
    return np.stack([legendre * quadrature, legendre]).astype(ml_dtypes.bfloat16)


def swap4(first, second):
    low = lax.broadcasted_iota(jnp.int32, first.shape, 1) < 4
    rolled_first, rolled_second = pltpu.roll(first, 4, 1), pltpu.roll(second, 4, 1)
    return jnp.where(low, first, rolled_second), jnp.where(low, rolled_first, second)


def pairs(tiles):
    split = tiles.reshape(8, 2, 8, 128)
    return split[:, 0], split[:, 1]


def fetch(source, target, sem):
    copy = pltpu.make_async_copy(source, target, sem)
    copy.start()
    return copy


def row_scale(values):
    return lax.rsqrt(jnp.sum(values * values, axis=-1, keepdims=True) * (1.0 / WIDTH) + EPS)


def bundle(noise_ref, keep_ref, gains_ref, params_ref):
    for f in range(FRAMES):
        level = jnp.full((8, 128), noise_ref[f], F32)
        params_ref[f] = lax.rsqrt(1.0 + level * level)
        params_ref[FRAMES + f] = jnp.full((8, 128), 0.0 if f == 0 else keep_ref[f], F32)
    for norm in range(3):
        for c in range(6):
            params_ref[2 * FRAMES + norm, c : c + 1, :] = gains_ref[
                norm : norm + 1, 128 * c : 128 * c + 128
            ]


def pack_window(window_ref, out_ref):
    for h in range(2):
        out_ref[:, 4 * h : 4 * h + 4] = window_ref[0:16, :, :, ATTN * h : ATTN * h + ATTN]
    for c in range(3):
        left = window_ref[16:18, :, :, 128 * c : 128 * c + 128].astype(F32).reshape(8, 8, 128)
        right = window_ref[16:18, :, :, ATTN + 128 * c : ATTN + 128 * c + 128].astype(F32)
        even, odd = swap4(left, right.reshape(8, 8, 128))
        for i in range(8):
            out_ref[2 * i, 8, :, 128 * c : 128 * c + 128] = even[i].astype(BF16)
            out_ref[2 * i + 1, 8, :, 128 * c : 128 * c + 128] = odd[i].astype(BF16)


def gain_row(params_ref, norm):
    return jnp.concatenate([params_ref[2 * FRAMES + norm, c : c + 1, :] for c in range(6)], 1)


def attend(params_ref, in_ref, w_any, out_ref, x_ref, proj_ref, w_ref, sems):
    w_copies = [fetch(w_any.at[:, cols], w_ref.at[:, cols], sems.at[b]) for b, cols in BLOCKS]
    scale = params_ref[0:FRAMES]
    gain = [params_ref[2 * FRAMES, c : c + 1, :].reshape(1, 1, 128) for c in range(6)]
    for s in range(4):
        parts = [
            in_ref[:, 4 * (c // 3) + s, :, 128 * (c % 3) : 128 * (c % 3) + 128].astype(F32) * scale
            for c in range(6)
        ]
        squares = sum(v * v for v in parts)
        r = lax.rsqrt(jnp.sum(squares, axis=-1, keepdims=True) * (1.0 / WIDTH) + EPS)
        for c in range(6):
            x_ref[128 * s : 128 * s + 128, 128 * c : 128 * c + 128] = (
                (parts[c] * r * gain[c]).reshape(128, 128).astype(BF16)
            )
    parts = [in_ref[:, 8, :, 128 * c : 128 * c + 128].astype(F32) * scale for c in range(3)]
    squares = sum(v * v for v in parts)
    total = jnp.broadcast_to(jnp.sum(squares, axis=-1, keepdims=True), squares.shape)
    r = lax.rsqrt((total + pltpu.roll(total, 4, 1)) * (1.0 / WIDTH) + EPS)
    low = lax.broadcasted_iota(jnp.int32, (1, 8, 128), 1) < 4
    for c in range(3):
        both = parts[c] * r * jnp.where(low, gain[c], gain[c + 3])
        left, right = swap4(*pairs(both))
        x_ref[512:576, 128 * c : 128 * c + 128] = left.reshape(64, 128).astype(BF16)
        x_ref[512:576, ATTN + 128 * c : ATTN + 128 * c + 128] = right.reshape(64, 128).astype(BF16)
    for b, cols in BLOCKS:
        w_copies[b].wait()
        proj_ref[:, cols] = jnp.dot(
            x_ref[...], w_ref[:, cols], preferred_element_type=F32
        ).astype(BF16)

    def mix(base, n):
        size = FRAMES * n
        row = lax.broadcasted_iota(jnp.int32, (1, size, size), 1)
        col = lax.broadcasted_iota(jnp.int32, (1, size, size), 2)
        kept = ((row & (n - 1)) == (col & (n - 1))) & (col // n <= row // n)
        lane = lax.broadcasted_iota(jnp.int32, (size, 128), 1) < 64
        one = jnp.where(lane, 1.0, 0.0).astype(BF16)
        other = jnp.where(lane, 0.0, 1.0).astype(BF16)
        results = []
        for h in range(3):
            q = proj_ref[base : base + size, 128 * h : 128 * h + 128]
            k = proj_ref[base : base + size, ATTN + 128 * h : ATTN + 128 * h + 128]
            v = proj_ref[base : base + size, 2 * ATTN + 128 * h : 2 * ATTN + 128 * h + 128]
            scores = lax.dot_general(
                jnp.concatenate([q * one, q * other], 0),
                k,
                (((1,), (1,)), ((), ())),
                preferred_element_type=F32,
            )
            scores = jnp.where(kept, scores.reshape(2, size, size) * 0.125, -1e30)
            expo = jnp.exp(scores - jnp.max(scores, axis=-1, keepdims=True))
            total = jnp.sum(expo, axis=-1, keepdims=True)
            weights = expo.reshape(2 * size, size).astype(BF16)
            mixed = jnp.dot(weights, v, preferred_element_type=F32).reshape(2, size, 128) / total
            results.append(jnp.where(lane, mixed[0], mixed[1]))
        return results

    for s in range(4):
        for h, mixed in enumerate(mix(128 * s, 8)):
            at = (s // 2) * 48 + 16 * h + 8 * (s % 2)
            mixed = mixed.reshape(FRAMES, 8, 128).astype(BF16)
            out_ref[0:15, at : at + 8, :] = mixed[1:16]
            out_ref[15:16, at : at + 8, :] = mixed[0:1]
    rest = [mixed.reshape(8, 8, 128) for mixed in mix(512, 4)]
    for at, (even, odd) in ((96, swap4(rest[0], rest[1])), (104, swap4(rest[2], rest[2]))):
        for i in range(8):
            out_ref[(2 * i - 1) % FRAMES, at : at + 8, :] = even[i].astype(BF16)
            out_ref[2 * i, at : at + 8, :] = odd[i].astype(BF16)


def put_chunks(columns, out_ref, out_any=None, sems=None):
    slot = lax.broadcasted_iota(jnp.int32, (LATS, 8, 128), 1)
    tiles, copies = [None, None], []
    for q in range(3):
        values = columns(q)
        for t in range(2):
            at = 32 * q + 16 * t
            block = values[:512, 128 * t : 128 * t + 128].reshape(LATS, 16, 128)
            out_ref[:, at : at + 16, :] = block.astype(BF16)
            part = values[512:, 128 * t : 128 * t + 128].reshape(LATS, 8, 128)
            tiles[t] = part if q == 0 else jnp.where(slot // 2 == q, part, tiles[t])
        if q == 2:
            for t in range(2):
                out_ref[:, 96 + 8 * t : 104 + 8 * t, :] = tiles[t].astype(BF16)
        rows = slice(32 * q, 32 * q + (32 if q < 2 else 48))
        if out_any is not None:
            copies.append(fetch(out_ref.at[:, rows, :], out_any.at[:, rows, :], sems.at[q]))
    return copies


def get_chunks(in_ref, rows_ref):
    for c in range(6):
        rows_ref[0:512, 128 * c : 128 * c + 128] = in_ref[:, 16 * c : 16 * c + 16, :].reshape(
            512, 128
        )
    slot = lax.broadcasted_iota(jnp.int32, (LATS, 8, 128), 1)
    for t in range(2):
        tile = in_ref[:, 96 + 8 * t : 104 + 8 * t, :].astype(F32)
        for q in range(3):
            at = 256 * q + 128 * t
            rows_ref[512:768, at : at + 128] = (
                jnp.where(slot // 2 == q, tile, 0.0).reshape(256, 128).astype(BF16)
            )


def to_spectra(
    frame_ref, params_ref, mixed_ref, window_any, w_any, tables_any,
    carry_any, out_any, out_ref, mixed_rows, base_rows, kept_ref, window_ref, w_ref, table_ref, sems, out_sems,
):
    w_copy = fetch(w_any, w_ref, sems.at[0])
    window_copy = fetch(window_any, window_ref, sems.at[1])
    table_copy = fetch(tables_any.at[0, :, 0:640], table_ref, sems.at[2])
    for block in range(2):
        for h in range(3):
            at = (block * 3 + h) * 16
            for d in range(FRAMES):
                mixed_rows[
                    32 * d + 16 * block : 32 * d + 16 * block + 16, 128 * h : 128 * h + 128
                ] = mixed_ref[d, at : at + 16, :]
    left, right = swap4(*pairs(mixed_ref[:, 96:104, :].astype(F32)))
    last, _ = swap4(*pairs(mixed_ref[:, 104:112, :].astype(F32)))
    for h, tile in enumerate((left, right, last)):
        mixed_rows[512:576, 128 * h : 128 * h + 128] = tile.reshape(64, 128).astype(BF16)
    scale = params_ref[frame_ref[0], 0:1, 0:1]
    gain = gain_row(params_ref, 1)
    w_copy.wait()
    window_copy.wait()
    first = window_ref[...].astype(F32) * scale + jnp.dot(
        mixed_rows[...], w_ref[...], preferred_element_type=F32
    )
    kept_ref[...] = first.astype(BF16)
    carries = [
        fetch(kept_ref, carry_any.at[0], sems.at[3]),
        fetch(window_ref, carry_any.at[1], sems.at[4]),
    ]
    base_rows[0:POINTS, :] = (first * row_scale(first) * gain).astype(BF16)
    base_rows[POINTS:640, :] = jnp.zeros((640 - POINTS, WIDTH), BF16)
    table_copy.wait()

    def columns(q):
        cols = slice(256 * q, 256 * q + 256)
        return jnp.dot(table_ref[...], base_rows[:, cols], preferred_element_type=F32)

    for copy in carries + put_chunks(columns, out_ref, out_any, out_sems):
        copy.wait()


def filter_orders(in_ref, down_ref, up_ref, out_ref, rows_ref, coeffs_ref):
    get_chunks(in_ref, rows_ref)
    degrees = 2 * ORDERS * LMAX
    factor = down_ref[degrees : degrees + LMAX, :].astype(F32)
    coeffs = jnp.dot(down_ref[0:degrees, :], rows_ref[...], preferred_element_type=F32)
    for b in range(2 * ORDERS):
        rows = slice(LMAX * b, LMAX * (b + 1))
        coeffs_ref[rows, :] = (coeffs[rows] * factor).astype(BF16)
    values = jnp.dot(up_ref[...], coeffs_ref[...], preferred_element_type=F32)
    put_chunks(lambda q: values[:, 256 * q : 256 * q + 256], out_ref)


def gelu(x):
    return 0.5 * x * (1.0 + jnp.tanh(np.float32(np.sqrt(2 / np.pi)) * (x + 0.044715 * (x * x * x))))


def feed_forward(
    frame_ref, params_ref, in_any, tables_any, carry_any, *refs
):
    shards, refs = refs[:SHARDS], refs[SHARDS:]
    (
        out_any, rows_ref, inner_ref, hidden_ref, out_ref, table_ref, carry_ref, second_ref,
        w_ref, in_ref, sems, w_sems,
    ) = refs
    in_copy = fetch(in_any, in_ref, sems.at[2])
    table_copy = fetch(tables_any.at[1, 0:POINTS], table_ref, sems.at[0])
    first_copy = fetch(carry_any.at[0], carry_ref.at[0], sems.at[1])
    in_copy.wait()
    get_chunks(in_ref, rows_ref)
    w_copies, at = [], 0
    for i, shard in enumerate(shards):
        w_copies.append(fetch(shard, w_ref.at[at : at + shard.shape[0]], w_sems.at[i]))
        at += shard.shape[0]
    gain = gain_row(params_ref, 2)
    table_copy.wait()
    second_ref[...] = jnp.dot(table_ref[...], rows_ref[...], preferred_element_type=F32)
    first_copy.wait()
    window_copy = fetch(carry_any.at[1], carry_ref.at[1], sems.at[4])
    second = carry_ref[0].astype(F32) + second_ref[...]
    second_ref[...] = second
    inner_ref[...] = (second * row_scale(second) * gain).astype(BF16)
    for b in range(2):
        units = slice(8 * b, 8 * b + 8)
        for copy in w_copies[4 * b : 4 * b + 4] if b == 0 else w_copies[4:]:
            copy.wait()
        raised = lax.dot_general(
            inner_ref[...],
            w_ref[units, 0:96, :].reshape(FF // 2, WIDTH),
            (((1,), (1,)), ((), ())),
            preferred_element_type=F32,
        )
        hidden_ref[:, FF // 2 * b : FF // 2 * (b + 1)] = gelu(raised).astype(BF16)
    ratio = params_ref[FRAMES + frame_ref[0], 0:1, 0:1]
    window_copy.wait()
    w_down = w_ref[:, 96:192, :].reshape(FF, WIDTH)
    copies = []
    for j in range(2):
        rows = slice(POINTS // 2 * j, POINTS // 2 * (j + 1))
        denoised = second_ref[rows, :] + jnp.dot(
            hidden_ref[rows, :], w_down, preferred_element_type=F32
        )
        state = carry_ref[1, rows, :].astype(F32)
        out_ref[rows, :] = (denoised + ratio * (state - denoised)).astype(BF16)
        copies.append(fetch(out_ref.at[rows], out_any.at[rows], sems.at[5 + j]))
    for copy in copies:
        copy.wait()


SPACES = {"v": pltpu.VMEM, "s": pltpu.SMEM, "h": pltpu.HBM}


def call(kernel, outs, kinds, scratch, args, flops, limit):
    specs = [pl.BlockSpec(memory_space=SPACES[kind]) for kind in kinds]
    return pl.pallas_call(
        kernel,
        out_shape=outs,
        in_specs=specs[: len(args)],
        out_specs=specs[len(args) :],
        scratch_shapes=[
            pltpu.VMEM(*entry) if isinstance(entry, tuple) else pltpu.SemaphoreType.DMA((entry,))
            for entry in scratch
        ],
        compiler_params=pltpu.CompilerParams(vmem_limit_bytes=int(limit * MIB)),
        cost_estimate=pl.CostEstimate(
            flops=flops,
            bytes_accessed=sum(a.size * a.dtype.itemsize for a in list(args) + outs),
            transcendentals=0,
        ),
    )(*args)


def exchange(chunks, axis):
    return lax.all_to_all(chunks, axis, split_axis=0, concat_axis=0, tiled=True)


def shift(value, steps):
    hops = [(source, (source + steps) % FRAMES) for source in range(FRAMES)]
    return lax.ppermute(value, "lead", hops)


def swap_cores(value):
    return lax.ppermute(value, "lead", [(source, source ^ 1) for source in range(FRAMES)])


def round_chips(value, chips):
    hops = [(s, (s + (2 * chips if s % 2 == 0 else -2 * chips)) % FRAMES) for s in range(FRAMES)]
    return lax.ppermute(value, "lead", hops)


def per_device(
    window, noise_level, keep_ratio, norm_gains, w_qkv, w_out, spectral_filter, w_in, w_down
):
    lead, lat = lax.axis_index("lead"), lax.axis_index("lat")
    frame = ((lead + 1) & (FRAMES - 1)).astype(jnp.int32).reshape(1)
    tables = jnp.asarray(fourier_tables())
    legendre = jnp.asarray(legendre_tables())
    placement = jnp.asarray(placement_table())
    shape = jax.ShapeDtypeStruct

    state = window.reshape(POINTS, WIDTH)
    (packed,) = call(
        pack_window,
        [shape((FRAMES, 9, 8, ATTN), BF16)],
        "vv",
        [],
        [window.reshape(18, 4, 8, WIDTH)],
        0,
        LIMITS[0],
    )
    ahead = shift(state, -1)
    packed, legendre, w_in, w_down, norm_gains = lax.optimization_barrier(
        (packed, legendre, w_in, w_down, norm_gains)
    )
    (params,) = call(
        bundle,
        [shape((2 * FRAMES + 3, 8, 128), F32)],
        "ssvv",
        [],
        [noise_level, keep_ratio, norm_gains],
        0,
        4,
    )
    own = jnp.concatenate([w_in, w_down], 0)[None]
    other = swap_cores(own)
    pair = jnp.where(
        lead % 2 == 0, jnp.concatenate([own, other], 0), jnp.concatenate([other, own], 0)
    )
    local = lax.dynamic_slice_in_dim(legendre, ORDERS * lat, ORDERS, 1)
    down = jnp.einsum("ilj,icjn->icln", local[0], placement, preferred_element_type=F32)
    down = down.astype(BF16).reshape(2 * ORDERS * LMAX, 768)
    down = jnp.concatenate([down, spectral_filter], 0)
    up = jnp.einsum("ilj,icjn->nicl", local[1], placement, preferred_element_type=F32)
    up = up.astype(BF16).reshape(768, 2 * ORDERS * LMAX)

    (mixed,) = call(
        attend,
        [shape((FRAMES, 112, 128), BF16)],
        "vvhv",
        [((POINTS, WIDTH), BF16), ((POINTS, 3 * ATTN), BF16), ((WIDTH, 3 * ATTN), BF16), 3],
        [params, exchange(packed, "lead"), w_qkv],
        2 * POINTS * WIDTH * 3 * ATTN,
        LIMITS[1],
    )
    mixed, ahead, pair = lax.optimization_barrier((mixed, ahead, pair))
    mixed = exchange(mixed, "lead")
    carry, spectra = call(
        to_spectra,
        [shape((2, POINTS, WIDTH), BF16), shape((LATS, 112, 128), BF16)],
        "svvhhhhh",
        [
            ((LATS, 112, 128), BF16),
            ((POINTS, ATTN), BF16),
            ((640, WIDTH), BF16),
            ((POINTS, WIDTH), BF16),
            ((POINTS, WIDTH), BF16),
            ((ATTN, WIDTH), BF16),
            ((768, 640), BF16),
            5,
            3,
        ],
        [frame, params, mixed, ahead, w_out, tables],
        2 * POINTS * WIDTH * (ATTN + 768),
        LIMITS[2],
    )
    spectra, pair = lax.optimization_barrier((spectra, pair))
    first_pair, second_pair = round_chips(pair, 1), round_chips(pair, 2)
    swapped = swap_cores(first_pair)
    by_order = exchange(spectra, "lat")
    by_order, second_pair, swapped = lax.optimization_barrier((by_order, second_pair, swapped))
    shards = [pair, first_pair, swapped, second_pair]
    (back,) = call(
        filter_orders,
        [shape((LATS, 112, 128), BF16)],
        "vvvv",
        [((768, WIDTH), BF16), ((2 * ORDERS * LMAX, WIDTH), BF16)],
        [by_order, down, up],
        4 * POINTS * WIDTH * 768,
        LIMITS[3],
    )
    back, second_pair = lax.optimization_barrier((back, second_pair))
    third_pair = round_chips(second_pair, 1)
    last = round_chips(jnp.where(lead % 2 == 0, second_pair[0:1], second_pair[1:2]), 2)
    shards += [third_pair, swap_cores(second_pair), swap_cores(third_pair), last, swap_cores(last)]
    (stepped,) = call(
        feed_forward,
        [shape((POINTS, WIDTH), BF16)],
        "svhhh" + "h" * SHARDS + "h",
        [
            ((768, WIDTH), BF16),
            ((POINTS, WIDTH), BF16),
            ((POINTS, FF), BF16),
            ((POINTS, WIDTH), BF16),
            ((POINTS, 768), BF16),
            ((2, POINTS, WIDTH), BF16),
            ((POINTS, WIDTH), F32),
            ((FRAMES, 192, WIDTH), BF16),
            ((LATS, 112, 128), BF16),
            7,
            SHARDS,
        ],
        [frame, params, exchange(back, "lat"), tables, carry, *shards],
        2 * POINTS * WIDTH * (2 * FF + 768),
        LIMITS[4],
    )
    return stepped.reshape(1, ROWS, NLON, WIDTH)


def solution(mesh):
    return jax.shard_map(
        per_device,
        mesh=mesh,
        in_specs=(
            P("lead", "lat", None, None),
            P(),
            P(),
            P(),
            P(),
            P(),
            P(),
            P("lead", None),
            P("lead", None),
        ),
        out_specs=P("lead", "lat", None, None),
        check_vma=False,
    )
```

```python
import jax
import jax.numpy as jnp
import ml_dtypes
import numpy as np
from jax import lax
from jax.experimental import pallas as pl
from jax.experimental.pallas import tpu as pltpu
from jax.sharding import PartitionSpec as P

F32, BF16 = jnp.float32, jnp.bfloat16
FRAMES, LATS, ROWS, NLON, NLAT, LMAX = 16, 32, 3, 192, 96, 96
POINTS, WIDTH, ATTN, FF = ROWS * NLON, 768, 384, 1536
ORDERS = LMAX // LATS
EPS = 1e-05
SHARDS = 9
BLOCKS = tuple((b, slice(ATTN * b, ATTN * (b + 1))) for b in range(3))
MIB = 1 << 20
LIMITS = (60, 51, 52, 16, 49)


def chunk_row(r):
    return r // 6, (r // 2) % 3, r % 2


def chunk_columns():
    listed = [(d,) + chunk_row(r) for d in range(LATS) for r in range(16)]
    for d in range(LATS):
        listed += [(d,) + chunk_row(16 + s % 2) if s < 6 else None for s in range(8)]
    return listed


def fourier_tables():
    forward = np.zeros((768, ROWS, NLON))
    inverse = np.zeros((768, ROWS, NLON))
    lon = np.arange(NLON)
    for at, entry in enumerate(chunk_columns()):
        if entry is None:
            continue
        owner, j, i, c = entry
        m = ORDERS * owner + i
        angle = 2 * np.pi * ((m * lon) % NLON) / NLON
        wave = np.cos(angle) if c == 0 else -np.sin(angle)
        forward[at, j] = wave
        inverse[at, j] = wave * (1.0 if m == 0 else 2.0)
    tables = np.zeros((2, 768, 768))
    tables[0, :, :POINTS] = forward.reshape(768, POINTS)
    tables[1, :POINTS] = inverse.reshape(768, POINTS).T
    return tables.astype(ml_dtypes.bfloat16)


def placement_table():
    table = np.zeros((ORDERS, 2, NLAT, 768))
    for at, entry in enumerate(chunk_columns()):
        if entry is not None:
            source, j, i, c = entry
            table[i, c, ROWS * source + j, at] = 1.0
    return table.astype(ml_dtypes.bfloat16)


def legendre_tables():
    colatitude = np.pi * (np.arange(NLAT) + 0.5) / NLAT
    cosines = np.cos(colatitude)
    sine_rows = np.sin(colatitude)
    legendre = np.zeros((LMAX, LMAX, NLAT))
    for order_m in range(LMAX):
        counter = np.arange(1, order_m + 1)
        log_part = (
            0.5 * np.log((2 * order_m + 1) / (4 * np.pi))
            + 0.5 * np.sum(np.log((2 * counter - 1) / (2 * counter)))
            + order_m * np.log(sine_rows)
        )
        diagonal_value = (-1.0) ** order_m * np.exp(log_part)
        legendre[order_m, order_m] = diagonal_value
        if order_m + 1 < LMAX:
            legendre[order_m, order_m + 1] = cosines * np.sqrt(2 * order_m + 3) * diagonal_value
        for degree_l in range(order_m + 2, LMAX):
            factor_a = np.sqrt(
                (4.0 * degree_l * degree_l - 1) / (degree_l * degree_l - order_m * order_m)
            )
            factor_b = np.sqrt(
                ((degree_l - 1.0) ** 2 - order_m * order_m) / (4.0 * (degree_l - 1) ** 2 - 1)
            )
            legendre[order_m, degree_l] = factor_a * (
                cosines * legendre[order_m, degree_l - 1]
                - factor_b * legendre[order_m, degree_l - 2]
            )
    quadrature = sine_rows * (np.pi / NLAT) * (2 * np.pi / NLON)
    return np.stack([legendre * quadrature, legendre]).astype(ml_dtypes.bfloat16)


def swap4(first, second):
    low = lax.broadcasted_iota(jnp.int32, first.shape, 1) < 4
    rolled_first, rolled_second = pltpu.roll(first, 4, 1), pltpu.roll(second, 4, 1)
    return jnp.where(low, first, rolled_second), jnp.where(low, rolled_first, second)


def pairs(tiles):
    split = tiles.reshape(8, 2, 8, 128)
    return split[:, 0], split[:, 1]


def fetch(source, target, sem):
    copy = pltpu.make_async_copy(source, target, sem)
    copy.start()
    return copy


def row_scale(values):
    return lax.rsqrt(jnp.sum(values * values, axis=-1, keepdims=True) * (1.0 / WIDTH) + EPS)


def bundle(noise_ref, keep_ref, gains_ref, params_ref):
    for f in range(FRAMES):
        level = jnp.full((8, 128), noise_ref[f], F32)
        params_ref[f] = lax.rsqrt(1.0 + level * level)
        params_ref[FRAMES + f] = jnp.full((8, 128), 0.0 if f == 0 else keep_ref[f], F32)
    for norm in range(3):
        for c in range(6):
            params_ref[2 * FRAMES + norm, c : c + 1, :] = gains_ref[
                norm : norm + 1, 128 * c : 128 * c + 128
            ]


def pack_window(window_ref, out_ref):
    for h in range(2):
        out_ref[:, 4 * h : 4 * h + 4] = window_ref[0:16, :, :, ATTN * h : ATTN * h + ATTN]
    for c in range(3):
        left = window_ref[16:18, :, :, 128 * c : 128 * c + 128].astype(F32).reshape(8, 8, 128)
        right = window_ref[16:18, :, :, ATTN + 128 * c : ATTN + 128 * c + 128].astype(F32)
        even, odd = swap4(left, right.reshape(8, 8, 128))
        for i in range(8):
            out_ref[2 * i, 8, :, 128 * c : 128 * c + 128] = even[i].astype(BF16)
            out_ref[2 * i + 1, 8, :, 128 * c : 128 * c + 128] = odd[i].astype(BF16)


def gain_row(params_ref, norm):
    return jnp.concatenate([params_ref[2 * FRAMES + norm, c : c + 1, :] for c in range(6)], 1)


def attend(params_ref, in_ref, w_any, out_ref, x_ref, proj_ref, w_ref, sems):
    w_copies = [fetch(w_any.at[:, cols], w_ref.at[:, cols], sems.at[b]) for b, cols in BLOCKS]
    scale = params_ref[0:FRAMES]
    gain = [params_ref[2 * FRAMES, c : c + 1, :].reshape(1, 1, 128) for c in range(6)]
    for s in range(4):
        parts = [
            in_ref[:, 4 * (c // 3) + s, :, 128 * (c % 3) : 128 * (c % 3) + 128].astype(F32) * scale
            for c in range(6)
        ]
        squares = sum(v * v for v in parts)
        r = lax.rsqrt(jnp.sum(squares, axis=-1, keepdims=True) * (1.0 / WIDTH) + EPS)
        for c in range(6):
            x_ref[128 * s : 128 * s + 128, 128 * c : 128 * c + 128] = (
                (parts[c] * r * gain[c]).reshape(128, 128).astype(BF16)
            )
    parts = [in_ref[:, 8, :, 128 * c : 128 * c + 128].astype(F32) * scale for c in range(3)]
    squares = sum(v * v for v in parts)
    total = jnp.broadcast_to(jnp.sum(squares, axis=-1, keepdims=True), squares.shape)
    r = lax.rsqrt((total + pltpu.roll(total, 4, 1)) * (1.0 / WIDTH) + EPS)
    low = lax.broadcasted_iota(jnp.int32, (1, 8, 128), 1) < 4
    for c in range(3):
        both = parts[c] * r * jnp.where(low, gain[c], gain[c + 3])
        left, right = swap4(*pairs(both))
        x_ref[512:576, 128 * c : 128 * c + 128] = left.reshape(64, 128).astype(BF16)
        x_ref[512:576, ATTN + 128 * c : ATTN + 128 * c + 128] = right.reshape(64, 128).astype(BF16)
    for b, cols in BLOCKS:
        w_copies[b].wait()
        proj_ref[:, cols] = jnp.dot(
            x_ref[...], w_ref[:, cols], preferred_element_type=F32
        ).astype(BF16)

    def mix(base, n):
        size = FRAMES * n
        row = lax.broadcasted_iota(jnp.int32, (1, size, size), 1)
        col = lax.broadcasted_iota(jnp.int32, (1, size, size), 2)
        kept = ((row & (n - 1)) == (col & (n - 1))) & (col // n <= row // n)
        lane = lax.broadcasted_iota(jnp.int32, (size, 128), 1) < 64
        one = jnp.where(lane, 1.0, 0.0).astype(BF16)
        other = jnp.where(lane, 0.0, 1.0).astype(BF16)
        results = []
        for h in range(3):
            q = proj_ref[base : base + size, 128 * h : 128 * h + 128]
            k = proj_ref[base : base + size, ATTN + 128 * h : ATTN + 128 * h + 128]
            v = proj_ref[base : base + size, 2 * ATTN + 128 * h : 2 * ATTN + 128 * h + 128]
            scores = lax.dot_general(
                jnp.concatenate([q * one, q * other], 0),
                k,
                (((1,), (1,)), ((), ())),
                preferred_element_type=F32,
            )
            scores = jnp.where(kept, scores.reshape(2, size, size) * 0.125, -1e30)
            expo = jnp.exp(scores - jnp.max(scores, axis=-1, keepdims=True))
            total = jnp.sum(expo, axis=-1, keepdims=True)
            weights = expo.reshape(2 * size, size).astype(BF16)
            mixed = jnp.dot(weights, v, preferred_element_type=F32).reshape(2, size, 128) / total
            results.append(jnp.where(lane, mixed[0], mixed[1]))
        return results

    for s in range(4):
        for h, mixed in enumerate(mix(128 * s, 8)):
            at = (s // 2) * 48 + 16 * h + 8 * (s % 2)
            mixed = mixed.reshape(FRAMES, 8, 128).astype(BF16)
            out_ref[0:15, at : at + 8, :] = mixed[1:16]
            out_ref[15:16, at : at + 8, :] = mixed[0:1]
    rest = [mixed.reshape(8, 8, 128) for mixed in mix(512, 4)]
    for at, (even, odd) in ((96, swap4(rest[0], rest[1])), (104, swap4(rest[2], rest[2]))):
        for i in range(8):
            out_ref[(2 * i - 1) % FRAMES, at : at + 8, :] = even[i].astype(BF16)
            out_ref[2 * i, at : at + 8, :] = odd[i].astype(BF16)


def put_chunks(columns, out_ref, out_any=None, sems=None):
    slot = lax.broadcasted_iota(jnp.int32, (LATS, 8, 128), 1)
    tiles, copies = [None, None], []
    for q in range(3):
        values = columns(q)
        for t in range(2):
            at = 32 * q + 16 * t
            block = values[:512, 128 * t : 128 * t + 128].reshape(LATS, 16, 128)
            out_ref[:, at : at + 16, :] = block.astype(BF16)
            part = values[512:, 128 * t : 128 * t + 128].reshape(LATS, 8, 128)
            tiles[t] = part if q == 0 else jnp.where(slot // 2 == q, part, tiles[t])
        if q == 2:
            for t in range(2):
                out_ref[:, 96 + 8 * t : 104 + 8 * t, :] = tiles[t].astype(BF16)
        rows = slice(32 * q, 32 * q + (32 if q < 2 else 48))
        if out_any is not None:
            copies.append(fetch(out_ref.at[:, rows, :], out_any.at[:, rows, :], sems.at[q]))
    return copies


def get_chunks(in_ref, rows_ref):
    for c in range(6):
        rows_ref[0:512, 128 * c : 128 * c + 128] = in_ref[:, 16 * c : 16 * c + 16, :].reshape(
            512, 128
        )
    slot = lax.broadcasted_iota(jnp.int32, (LATS, 8, 128), 1)
    for t in range(2):
        tile = in_ref[:, 96 + 8 * t : 104 + 8 * t, :].astype(F32)
        for q in range(3):
            at = 256 * q + 128 * t
            rows_ref[512:768, at : at + 128] = (
                jnp.where(slot // 2 == q, tile, 0.0).reshape(256, 128).astype(BF16)
            )


def to_spectra(
    frame_ref, params_ref, mixed_ref, window_any, w_any, tables_any,
    carry_any, out_any, out_ref, mixed_rows, base_rows, kept_ref, window_ref, w_ref, table_ref, sems, out_sems,
):
    w_copy = fetch(w_any, w_ref, sems.at[0])
    window_copy = fetch(window_any, window_ref, sems.at[1])
    table_copy = fetch(tables_any.at[0, :, 0:640], table_ref, sems.at[2])
    for block in range(2):
        for h in range(3):
            at = (block * 3 + h) * 16
            for d in range(FRAMES):
                mixed_rows[
                    32 * d + 16 * block : 32 * d + 16 * block + 16, 128 * h : 128 * h + 128
                ] = mixed_ref[d, at : at + 16, :]
    left, right = swap4(*pairs(mixed_ref[:, 96:104, :].astype(F32)))
    last, _ = swap4(*pairs(mixed_ref[:, 104:112, :].astype(F32)))
    for h, tile in enumerate((left, right, last)):
        mixed_rows[512:576, 128 * h : 128 * h + 128] = tile.reshape(64, 128).astype(BF16)
    scale = params_ref[frame_ref[0], 0:1, 0:1]
    gain = gain_row(params_ref, 1)
    w_copy.wait()
    window_copy.wait()
    first = window_ref[...].astype(F32) * scale + jnp.dot(
        mixed_rows[...], w_ref[...], preferred_element_type=F32
    )
    kept_ref[...] = first.astype(BF16)
    carries = [
        fetch(kept_ref, carry_any.at[0], sems.at[3]),
        fetch(window_ref, carry_any.at[1], sems.at[4]),
    ]
    base_rows[0:POINTS, :] = (first * row_scale(first) * gain).astype(BF16)
    base_rows[POINTS:640, :] = jnp.zeros((640 - POINTS, WIDTH), BF16)
    table_copy.wait()

    def columns(q):
        cols = slice(256 * q, 256 * q + 256)
        return jnp.dot(table_ref[...], base_rows[:, cols], preferred_element_type=F32)

    for copy in carries + put_chunks(columns, out_ref, out_any, out_sems):
        copy.wait()


def filter_orders(in_ref, down_ref, up_ref, out_ref, rows_ref, coeffs_ref):
    get_chunks(in_ref, rows_ref)
    degrees = 2 * ORDERS * LMAX
    factor = down_ref[degrees : degrees + LMAX, :].astype(F32)
    coeffs = jnp.dot(down_ref[0:degrees, :], rows_ref[...], preferred_element_type=F32)
    for b in range(2 * ORDERS):
        rows = slice(LMAX * b, LMAX * (b + 1))
        coeffs_ref[rows, :] = (coeffs[rows] * factor).astype(BF16)
    values = jnp.dot(up_ref[...], coeffs_ref[...], preferred_element_type=F32)
    put_chunks(lambda q: values[:, 256 * q : 256 * q + 256], out_ref)


def gelu(x):
    return 0.5 * x * (1.0 + jnp.tanh(np.float32(np.sqrt(2 / np.pi)) * (x + 0.044715 * (x * x * x))))


def feed_forward(
    frame_ref, params_ref, in_any, tables_any, carry_any, *refs
):
    shards, refs = refs[:SHARDS], refs[SHARDS:]
    (
        out_any, rows_ref, inner_ref, hidden_ref, out_ref, table_ref, carry_ref, second_ref,
        w_ref, in_ref, sems, w_sems,
    ) = refs
    in_copy = fetch(in_any, in_ref, sems.at[2])
    table_copy = fetch(tables_any.at[1, 0:POINTS], table_ref, sems.at[0])
    first_copy = fetch(carry_any.at[0], carry_ref.at[0], sems.at[1])
    in_copy.wait()
    get_chunks(in_ref, rows_ref)
    w_copies, at = [], 0
    for i, shard in enumerate(shards):
        w_copies.append(fetch(shard, w_ref.at[at : at + shard.shape[0]], w_sems.at[i]))
        at += shard.shape[0]
    gain = gain_row(params_ref, 2)
    table_copy.wait()
    second_ref[...] = jnp.dot(table_ref[...], rows_ref[...], preferred_element_type=F32)
    first_copy.wait()
    window_copy = fetch(carry_any.at[1], carry_ref.at[1], sems.at[4])
    second = carry_ref[0].astype(F32) + second_ref[...]
    second_ref[...] = second
    inner_ref[...] = (second * row_scale(second) * gain).astype(BF16)
    for b in range(2):
        units = slice(8 * b, 8 * b + 8)
        for copy in w_copies[4 * b : 4 * b + 4] if b == 0 else w_copies[4:]:
            copy.wait()
        raised = lax.dot_general(
            inner_ref[...],
            w_ref[units, 0:96, :].reshape(FF // 2, WIDTH),
            (((1,), (1,)), ((), ())),
            preferred_element_type=F32,
        )
        hidden_ref[:, FF // 2 * b : FF // 2 * (b + 1)] = gelu(raised).astype(BF16)
    ratio = params_ref[FRAMES + frame_ref[0], 0:1, 0:1]
    window_copy.wait()
    w_down = w_ref[:, 96:192, :].reshape(FF, WIDTH)
    copies = []
    for j in range(2):
        rows = slice(POINTS // 2 * j, POINTS // 2 * (j + 1))
        denoised = second_ref[rows, :] + jnp.dot(
            hidden_ref[rows, :], w_down, preferred_element_type=F32
        )
        state = carry_ref[1, rows, :].astype(F32)
        out_ref[rows, :] = (denoised + ratio * (state - denoised)).astype(BF16)
        copies.append(fetch(out_ref.at[rows], out_any.at[rows], sems.at[5 + j]))
    for copy in copies:
        copy.wait()


SPACES = {"v": pltpu.VMEM, "s": pltpu.SMEM, "h": pltpu.HBM}


def call(kernel, outs, kinds, scratch, args, flops, limit):
    specs = [pl.BlockSpec(memory_space=SPACES[kind]) for kind in kinds]
    return pl.pallas_call(
        kernel,
        out_shape=outs,
        in_specs=specs[: len(args)],
        out_specs=specs[len(args) :],
        scratch_shapes=[
            pltpu.VMEM(*entry) if isinstance(entry, tuple) else pltpu.SemaphoreType.DMA((entry,))
            for entry in scratch
        ],
        compiler_params=pltpu.CompilerParams(vmem_limit_bytes=int(limit * MIB)),
        cost_estimate=pl.CostEstimate(
            flops=flops,
            bytes_accessed=sum(a.size * a.dtype.itemsize for a in list(args) + outs),
            transcendentals=0,
        ),
    )(*args)


def exchange(chunks, axis):
    return lax.all_to_all(chunks, axis, split_axis=0, concat_axis=0, tiled=True)


def shift(value, steps):
    hops = [(source, (source + steps) % FRAMES) for source in range(FRAMES)]
    return lax.ppermute(value, "lead", hops)


def swap_cores(value):
    return lax.ppermute(value, "lead", [(source, source ^ 1) for source in range(FRAMES)])


def round_chips(value, chips):
    hops = [(s, (s + (2 * chips if s % 2 == 0 else -2 * chips)) % FRAMES) for s in range(FRAMES)]
    return lax.ppermute(value, "lead", hops)


def per_device(
    window, noise_level, keep_ratio, norm_gains, w_qkv, w_out, spectral_filter, w_in, w_down
):
    lead, lat = lax.axis_index("lead"), lax.axis_index("lat")
    frame = ((lead + 1) & (FRAMES - 1)).astype(jnp.int32).reshape(1)
    tables = jnp.asarray(fourier_tables())
    legendre = jnp.asarray(legendre_tables())
    placement = jnp.asarray(placement_table())
    shape = jax.ShapeDtypeStruct

    state = window.reshape(POINTS, WIDTH)
    (packed,) = call(
        pack_window,
        [shape((FRAMES, 9, 8, ATTN), BF16)],
        "vv",
        [],
        [window.reshape(18, 4, 8, WIDTH)],
        0,
        LIMITS[0],
    )
    ahead = shift(state, -1)
    packed, legendre, w_in, w_down, norm_gains = lax.optimization_barrier(
        (packed, legendre, w_in, w_down, norm_gains)
    )
    (params,) = call(
        bundle,
        [shape((2 * FRAMES + 3, 8, 128), F32)],
        "ssvv",
        [],
        [noise_level, keep_ratio, norm_gains],
        0,
        4,
    )
    own = jnp.concatenate([w_in, w_down], 0)[None]
    pair = jnp.concatenate([own, swap_cores(own)], 0)
    local = lax.dynamic_slice_in_dim(legendre, ORDERS * lat, ORDERS, 1)
    down = jnp.einsum("ilj,icjn->icln", local[0], placement, preferred_element_type=F32)
    down = down.astype(BF16).reshape(2 * ORDERS * LMAX, 768)
    down = jnp.concatenate([down, spectral_filter], 0)
    up = jnp.einsum("ilj,icjn->nicl", local[1], placement, preferred_element_type=F32)
    up = up.astype(BF16).reshape(768, 2 * ORDERS * LMAX)

    (mixed,) = call(
        attend,
        [shape((FRAMES, 112, 128), BF16)],
        "vvhv",
        [((POINTS, WIDTH), BF16), ((POINTS, 3 * ATTN), BF16), ((WIDTH, 3 * ATTN), BF16), 3],
        [params, exchange(packed, "lead"), w_qkv],
        2 * POINTS * WIDTH * 3 * ATTN,
        LIMITS[1],
    )
    mixed, ahead, pair = lax.optimization_barrier((mixed, ahead, pair))
    mixed = exchange(mixed, "lead")
    carry, spectra = call(
        to_spectra,
        [shape((2, POINTS, WIDTH), BF16), shape((LATS, 112, 128), BF16)],
        "svvhhhhh",
        [
            ((LATS, 112, 128), BF16),
            ((POINTS, ATTN), BF16),
            ((640, WIDTH), BF16),
            ((POINTS, WIDTH), BF16),
            ((POINTS, WIDTH), BF16),
            ((ATTN, WIDTH), BF16),
            ((768, 640), BF16),
            5,
            3,
        ],
        [frame, params, mixed, ahead, w_out, tables],
        2 * POINTS * WIDTH * (ATTN + 768),
        LIMITS[2],
    )
    spectra, pair = lax.optimization_barrier((spectra, pair))
    first_pair, second_pair = round_chips(pair, 1), round_chips(pair, 2)
    swapped = swap_cores(first_pair)
    by_order = exchange(spectra, "lat")
    by_order, second_pair, swapped = lax.optimization_barrier((by_order, second_pair, swapped))
    shards = [pair, first_pair, swapped, second_pair]
    (back,) = call(
        filter_orders,
        [shape((LATS, 112, 128), BF16)],
        "vvvv",
        [((768, WIDTH), BF16), ((2 * ORDERS * LMAX, WIDTH), BF16)],
        [by_order, down, up],
        4 * POINTS * WIDTH * 768,
        LIMITS[3],
    )
    back, second_pair = lax.optimization_barrier((back, second_pair))
    third_pair = round_chips(second_pair, 1)
    last = round_chips(second_pair[0:1], 2)
    shards += [third_pair, swap_cores(second_pair), swap_cores(third_pair), last, swap_cores(last)]
    (stepped,) = call(
        feed_forward,
        [shape((POINTS, WIDTH), BF16)],
        "svhhh" + "h" * SHARDS + "h",
        [
            ((768, WIDTH), BF16),
            ((POINTS, WIDTH), BF16),
            ((POINTS, FF), BF16),
            ((POINTS, WIDTH), BF16),
            ((POINTS, 768), BF16),
            ((2, POINTS, WIDTH), BF16),
            ((POINTS, WIDTH), F32),
            ((FRAMES, 192, WIDTH), BF16),
            ((LATS, 112, 128), BF16),
            7,
            SHARDS,
        ],
        [frame, params, exchange(back, "lat"), tables, carry, *shards],
        2 * POINTS * WIDTH * (2 * FF + 768),
        LIMITS[4],
    )
    return stepped.reshape(1, ROWS, NLON, WIDTH)


def solution(mesh):
    return jax.shard_map(
        per_device,
        mesh=mesh,
        in_specs=(
            P("lead", "lat", None, None),
            P(),
            P(),
            P(),
            P(),
            P(),
            P(),
            P("lead", None),
            P("lead", None),
        ),
        out_specs=P("lead", "lat", None, None),
        check_vma=False,
    )
```
